256 devices in a mesh: row: 8 (over y, z_hi), col: 32 (over z_lo, x, core).
Axes of the slice: x: 4, y: 4, z: 8 (z_hi: 2, z_lo: 4; z = z_hi * 4 + z_lo), core: 2. Of those that a mesh axis runs over, the one named last changes fastest.
Arguments:
- features: bfloat16 [262144, 128], P(('col', 'row')), may hold values from -6 to 6
- weight: bfloat16 [128, 128], replicated, may hold values from -0.5 to 0.5
- tile_values: bfloat16 [8, 32, 64, 128, 128], P('row', 'col'), may hold values from -0.25 to 0.25
- tile_rows: int32 [8, 32, 64], P('row', 'col'), may hold values from 0 to 255, as said below
- tile_cols: int32 [8, 32, 64], P('row', 'col'), may hold values from 0 to 63
- tile_live: int32 [8, 32], P('row', 'col'), may hold values from 8 to 64, as said below
- cotangent: bfloat16 [262144, 128], P(('row', 'col')), may hold values from -6 to 6
Outputs:
- layer_out: bfloat16 [262144, 128], P(('row', 'col'))
- grad_x: bfloat16 [262144, 128], P(('col', 'row'))
- grad_w: float32 [128, 128], replicated
The draws below stay inside these ranges and needn't reach their ends.
Inputs may be any that keep to these rules, and one draw needn't show every extreme that they name: `tile_live`: slots at or beyond a device's count are ignored; some device has all 64 slots live, and each count is 64 divided by 1, 2, 4 or 8. `tile_rows`: over all 64 slots of one device, at most 4 name block rows c * 8 to c * 8 + 7 for any one c; in every grid row some c receives exactly 4 such slots from every device of that row, and these are the devices' first slots.
All inputs are finite; a program needn't handle non-finite values.
Results may differ from the reference program's by a relative error of at most 0.022.
Values may be sent and summed in bfloat16 or wider, within the bound.
A program may use at most 64 MiB of HBM per device.

```python
import jax
import jax.numpy as jnp
from jax import lax

F = 128
TILE = 128
NB_DEV = 8
TILES_DEV = 64
NODES = 262144
N_ROW = 8
N_COL = 32


def draw_tile_live(key, part):
    key = jax.random.fold_in(key, 7)
    first_key, second_key = jax.random.split(key)
    shifts = jax.random.randint(first_key, (N_ROW * N_COL,), 0, 4).astype(jnp.int32)
    counts = jnp.right_shift(jnp.full((N_ROW * N_COL,), TILES_DEV, jnp.int32), shifts)
    chosen = jax.random.randint(second_key, (), 0, N_ROW * N_COL)
    counts = counts.at[chosen].set(TILES_DEV)
    return counts.reshape(N_ROW, N_COL).astype(jnp.int32)


def draw_tile_rows(key, part):
    key = jax.random.fold_in(key, 11)
    hot_key, perm_key, offset_key = jax.random.split(key, 3)
    per_dest = 2 * TILES_DEV // N_COL
    slot_total = N_COL * per_dest
    hot_rows = jax.random.randint(hot_key, (N_ROW,), 0, N_COL).astype(jnp.int32)
    hot_dev = jnp.repeat(hot_rows, N_COL)
    perm_keys = jax.random.split(perm_key, N_ROW * N_COL)
    perms = jax.vmap(lambda single: jax.random.permutation(single, slot_total))(perm_keys).astype(jnp.int32)
    away = (perms // per_dest != hot_dev[:, None]).astype(jnp.int32)
    order = jnp.argsort(away, axis=-1, stable=True)
    taken = jnp.take_along_axis(perms, order, axis=-1)[:, :TILES_DEV]
    dest = taken // per_dest
    offsets = jax.random.randint(offset_key, dest.shape, 0, NB_DEV).astype(jnp.int32)
    rows = dest * NB_DEV + offsets
    return rows.reshape(N_ROW, N_COL, TILES_DEV).astype(jnp.int32)


def touch_ends(array, rng, smallest, largest):
    spot = [jax.random.randint(jax.random.fold_in(rng, axis), (), 0, length) for axis, length in enumerate(array.shape)]
    widest = array.shape.index(max(array.shape))
    next_to = spot[:widest] + [(spot[widest] + 1) % array.shape[widest]] + spot[widest + 1:]
    return array.at[tuple(spot)].set(smallest).at[tuple(next_to)].set(largest)


def shard_levels(key, shape, cuts, low, high):
    gain = 1.0
    for dim, shards_of in cuts:
        draws = jax.random.uniform(jax.random.fold_in(jax.random.fold_in(key, 6), dim), (shards_of,), jnp.float32, low / len(cuts), high / len(cuts))
        gain = gain * jnp.repeat(jnp.exp(draws), shape[dim] // shards_of).reshape((-1,) + (1,) * (len(shape) - 1 - dim))
    return gain


def centred(key, extent, width, limit, shards=(), kind=jnp.bfloat16):
    array = jax.random.normal(key, extent, jnp.float32) * width
    if len(shards) > 0:
        array = shard_levels(key, extent, shards, -0.22, 0.18) * array
    return jnp.clip(array, min=-limit, max=limit).astype(kind)


def setup_inputs(seed: int = 0) -> dict:
    key_of = jax.random.split(jax.random.key(seed), 8)
    features = centred(key_of[0], (NODES, F), 1.0, 6.0, ((0, 256),))
    weight = centred(key_of[1], (F, F), F ** -0.5, 0.5)
    tile_values = centred(key_of[2], (N_ROW, N_COL, TILES_DEV, TILE, TILE), (TILE * TILES_DEV // (2 * NB_DEV)) ** -0.5, 0.25, ((0, 8), (1, 32)))
    tile_rows = draw_tile_rows(jax.random.fold_in(key_of[7], 71), 0)
    tile_cols = touch_ends(jax.random.randint(key_of[4], (N_ROW, N_COL, TILES_DEV), 0, NB_DEV * N_ROW), jax.random.fold_in(key_of[4], 1), 0, (NB_DEV * N_ROW) - 1).astype(jnp.int32)
    tile_live = draw_tile_live(jax.random.fold_in(key_of[7], 71), 0)
    cotangent = centred(key_of[6], (NODES, F), 1.0, 6.0, ((0, 256),))
    return {"features": features, "weight": weight, "tile_values": tile_values, "tile_rows": tile_rows, "tile_cols": tile_cols, "tile_live": tile_live, "cotangent": cotangent}


def silu_slope(value):
    sigma = jax.nn.sigmoid(value)
    return sigma * (1.0 + value * (1.0 - sigma))


def reference(features, weight, tile_values, tile_rows, tile_cols, tile_live, cotangent):
    count_dev = N_ROW * N_COL
    projected = jnp.dot(features, weight, preferred_element_type=jnp.float32).astype(jnp.bfloat16)
    blocks_proj = projected.reshape(-1, TILE, F)
    entries_all = tile_values.reshape(count_dev, TILES_DEV, TILE, TILE)
    rows_all = tile_rows.reshape(count_dev, TILES_DEV).astype(jnp.int32)
    cols_all = tile_cols.reshape(count_dev, TILES_DEV).astype(jnp.int32)
    live_all = tile_live.reshape(count_dev).astype(jnp.int32)
    device_ids = jnp.arange(count_dev, dtype=jnp.int32)
    row_start = (device_ids // N_COL) * (NB_DEV * N_COL)
    col_start = (device_ids % N_COL) * (NB_DEV * N_ROW)
    slot_index = jnp.arange(TILES_DEV, dtype=jnp.int32)

    def forward_step(accumulated, inputs):
        entries, row_index, col_index, live_count, row_base, col_base = inputs
        keep_tile = (slot_index < live_count).astype(jnp.float32)
        source = blocks_proj[col_index + col_base].astype(jnp.float32)
        product = jnp.einsum('tij,tjf->tif', entries.astype(jnp.float32), source)
        product = product * keep_tile[:, None, None]
        return accumulated.at[row_index + row_base].add(product), None

    start_blocks = jnp.zeros(blocks_proj.shape, jnp.float32)
    preact, _ = lax.scan(forward_step, start_blocks, (entries_all, rows_all, cols_all, live_all, row_start, col_start))
    preact = preact.reshape(-1, F)
    layer_out = jax.nn.silu(preact).astype(jnp.bfloat16)
    grad_pre = (cotangent.astype(jnp.float32) * silu_slope(preact)).astype(jnp.bfloat16)
    blocks_grad = grad_pre.reshape(-1, TILE, F)

    def backward_step(accumulated, inputs):
        entries, row_index, col_index, live_count, row_base, col_base = inputs
        keep_tile = (slot_index < live_count).astype(jnp.float32)
        source = blocks_grad[row_index + row_base].astype(jnp.float32)
        product = jnp.einsum('tij,tif->tjf', entries.astype(jnp.float32), source)
        product = product * keep_tile[:, None, None]
        return accumulated.at[col_index + col_base].add(product), None

    grad_proj, _ = lax.scan(backward_step, jnp.zeros(blocks_grad.shape, jnp.float32), (entries_all, rows_all, cols_all, live_all, row_start, col_start))
    grad_proj = grad_proj.reshape(-1, F)
    grad_w = jnp.dot(features.astype(jnp.float32).T, grad_proj, precision=lax.Precision.HIGHEST)
    grad_x = jnp.dot(grad_proj, weight.astype(jnp.float32).T, precision=lax.Precision.HIGHEST).astype(jnp.bfloat16)
    return (layer_out, grad_x, grad_w)
```

```python
import functools

import jax
import jax.numpy as jnp
from jax import lax
from jax.experimental import pallas as pl
from jax.experimental.pallas import tpu as pltpu
from jax.sharding import PartitionSpec as P

MESH = pl.DeviceIdType.MESH
F32 = jnp.float32
BF16 = jnp.bfloat16
ROWS = 1024
VMEM_BYTES = 56 << 20


def place():
    r, c = lax.axis_index("row"), lax.axis_index("col")
    return (c // 2) % 4, r // 2, r % 2, c // 8, c % 2


def device(x, y, zh, zl, k):
    return (y * 2 + zh, zl * 8 + x * 2 + k)


def remote(src, dst, send, recv, target):
    return pltpu.make_async_remote_copy(
        src_ref=src, dst_ref=dst, send_sem=send, recv_sem=recv, device_id=target, device_id_type=MESH
    )


def greet(partners):
    barrier = pltpu.get_barrier_semaphore()
    for partner in partners:
        pl.semaphore_signal(barrier, inc=1, device_id=partner, device_id_type=MESH)
    pl.semaphore_wait(barrier, len(partners))


class Sends:
    def __init__(self, send_sems):
        self.sems = send_sems
        self.started = []

    def start(self, src, dst, recv, target):
        copy = remote(src, dst, self.sems.at[len(self.started)], recv, target)
        copy.start()
        self.started.append(copy)

    def finish(self):
        for copy in self.started:
            copy.wait_send()


def arrived(ref, recv, me):
    remote(ref, ref, recv, recv, me).wait_recv()


def each_chunk(rows, step, body):
    def go(i, carry):
        body(pl.ds(pl.multiple_of(i * step, step), step))
        return carry

    lax.fori_loop(0, rows // step, go, 0)


def add_into(out, terms, rows, step=128):
    def body(at):
        total = out[at, :].astype(F32)
        for term in terms:
            total = total + term[at, :].astype(F32)
        out[at, :] = total.astype(out.dtype)

    each_chunk(rows, step, body)


G1_PIECES = 4
G1_ROWS = ROWS * 2 // G1_PIECES


def gather_row_kernel(x_ref, out_ref, local_sem, send_sems, z_sems, near_sems, far_sems):
    x, y, zh, zl, k = place()
    right, left = device(x, (y + 1) % 4, zh, zl, k), device(x, (y + 3) % 4, zh, zl, k)
    over = device(x, y, 1 - zh, zl, k)
    greet([right, left, over])
    sends = Sends(send_sems)
    own = y * 2 + zh
    half = G1_ROWS // 2
    per = G1_PIECES // 2

    def piece(yy, p, part=None):
        block = (yy % 4) * 2 + (zh if p < per else 1 - zh)
        start, size = (p % per) * G1_ROWS, G1_ROWS
        if part is not None:
            start, size = start + part * half, half
        return out_ref.at[block, pl.ds(start, size)]

    mine = pltpu.make_async_copy(x_ref, out_ref.at[own], local_sem)
    mine.start()
    for p in range(per):
        sends.start(x_ref.at[pl.ds(p * G1_ROWS, G1_ROWS)], piece(y, p), z_sems.at[p], over)
    for p in range(per):
        src = x_ref.at[pl.ds(p * G1_ROWS, G1_ROWS)]
        sends.start(src, piece(y, p), near_sems.at[p, 0], right)
        sends.start(src, piece(y, p), near_sems.at[p, 1], left)

    def spread(p):
        here = piece(y, p)
        arrived(here, z_sems.at[p - per], over)
        sends.start(here, here, near_sems.at[p, 0], right)
        sends.start(here, here, near_sems.at[p, 1], left)

    def forward(p):
        arrived(piece(y + 3, p), near_sems.at[p, 0], left)
        src = piece(y + 3, p, 0)
        sends.start(src, src, far_sems.at[p, 0], right)
        arrived(piece(y + 1, p), near_sems.at[p, 1], right)
        src = piece(y + 1, p, 1)
        sends.start(src, src, far_sems.at[p, 1], left)

    for p in range(per):
        forward(p)
        spread(per + p)
    for p in range(per):
        forward(per + p)
    for p in range(G1_PIECES):
        arrived(piece(y + 2, p, 0), far_sems.at[p, 0], left)
        arrived(piece(y + 2, p, 1), far_sems.at[p, 1], right)
    sends.finish()
    mine.wait()


def gather_row(features):
    return pl.pallas_call(
        gather_row_kernel,
        out_shape=jax.ShapeDtypeStruct((8, ROWS, 128), BF16),
        in_specs=[pl.BlockSpec(memory_space=pl.ANY)],
        out_specs=pl.BlockSpec(memory_space=pl.ANY),
        scratch_shapes=[
            pltpu.SemaphoreType.DMA,
            pltpu.SemaphoreType.DMA((G1_PIECES // 2 + 4 * G1_PIECES,)),
            pltpu.SemaphoreType.DMA((G1_PIECES // 2,)),
            pltpu.SemaphoreType.DMA((G1_PIECES, 2)),
            pltpu.SemaphoreType.DMA((G1_PIECES, 2)),
        ],
        compiler_params=pltpu.CompilerParams(
            collective_id=1, has_side_effects=True, vmem_limit_bytes=VMEM_BYTES
        ),
    )(features)


TURN = 4


def forward_kernel(rows_ref, cols_ref, live_ref, x_ref, w_ref, tiles_ref, out_ref, xv, proj, tiles, acc, sems):
    load_x = pltpu.make_async_copy(x_ref, xv, sems.at[0])
    load_t = pltpu.make_async_copy(tiles_ref, tiles, sems.at[1])
    load_x.start()
    load_t.start()

    def clear(i, carry):
        acc[pl.ds(i * 4, 4)] = jnp.zeros((4, 128, 128), BF16)
        return carry

    lax.fori_loop(0, 64, clear, 0)
    load_x.wait()
    weight = w_ref[...]

    def project(i, carry):
        block = xv[pl.ds(pl.multiple_of(i * 512, 512), 512), :]
        value = jnp.dot(block, weight, preferred_element_type=F32).astype(BF16)
        proj[pl.ds(i * 4, 4)] = value.reshape(4, 128, 128)
        return carry

    lax.fori_loop(0, 16, project, 0)
    load_t.wait()

    def turn(i, carry):
        products = []
        for u in range(TURN):
            s = i * TURN + u
            products.append(jnp.dot(tiles[s], proj[cols_ref[s]], preferred_element_type=F32))
        for u in range(TURN):
            b = rows_ref[i * TURN + u]
            acc[b] = (acc[b].astype(F32) + products[u]).astype(BF16)
        return carry

    lax.fori_loop(0, live_ref[0] // TURN, turn, 0)
    store = pltpu.make_async_copy(acc, out_ref, sems.at[2])
    store.start()
    store.wait()


def forward(rows, cols, live, x, weight, tiles):
    smem, vmem, anywhere = (pl.BlockSpec(memory_space=m) for m in (pltpu.SMEM, pltpu.VMEM, pl.ANY))
    return pl.pallas_call(
        forward_kernel,
        out_shape=jax.ShapeDtypeStruct((256, 128, 128), BF16),
        in_specs=[smem, smem, smem, anywhere, vmem, anywhere],
        out_specs=anywhere,
        scratch_shapes=[
            pltpu.VMEM((8 * ROWS, 128), BF16),
            pltpu.VMEM((64, 128, 128), BF16),
            pltpu.VMEM((64, 128, 128), BF16),
            pltpu.VMEM((256, 128, 128), BF16),
            pltpu.SemaphoreType.DMA((3,)),
        ],
        compiler_params=pltpu.CompilerParams(vmem_limit_bytes=VMEM_BYTES),
    )(rows, cols, live, x, weight, tiles)


ORDER = (2, 1, 3, 0)
HALF = ROWS // 2
H1, H2 = pl.ds(0, HALF), pl.ds(HALF, HALF)


def middle_kernel(
    part_ref, cot_ref, layer_ref, grows_ref,
    own, sib, s1, s2, zin, gown,
    load_sems, sib_sems, s1_sems, s2_sems, z_sems, send_sems,
    gz_sems, gnear_sems, gfar_sems, gsib_sems,
):
    x, y, zh, zl, k = place()
    me = device(x, y, zh, zl, k)
    right, left = device((x + 1) % 4, y, zh, zl, k), device((x + 3) % 4, y, zh, zl, k)
    sibling = device(x, y, zh, zl, 1 - k)
    along = [None] + [device(x, y, zh, (zl + j) % 4, k) for j in range(1, 4)]
    loads = {}
    for j in ORDER:
        for m in (2, 1, 3, 0):
            c = ((zl + j) % 4) * 8 + ((x + m) % 4) * 2 + k
            loads[j, m] = pltpu.make_async_copy(part_ref.at[c], own.at[j, m], load_sems.at[j, m])
            loads[j, m].start()
    greet([right, left, sibling] + along[1:])
    sends = Sends(send_sems)
    for j in ORDER:
        for m in (2, 1, 3, 0):
            c = ((zl + j) % 4) * 8 + ((x + m) % 4) * 2 + (1 - k)
            sends.start(part_ref.at[c], sib.at[j, m], sib_sems.at[j, m], sibling)

    def joined(j, m):
        loads[j, m].wait()
        arrived(sib.at[j, m], sib_sems.at[j, m], sibling)

    def step_a(j):
        joined(j, 2)
        add_into(own.at[j, 2], [sib.at[j, 2]], ROWS)
        sends.start(own.at[j, 2, H1], s1.at[j, 0], s1_sems.at[j, 0], right)
        sends.start(own.at[j, 2, H2], s1.at[j, 1], s1_sems.at[j, 1], left)

    def step_b(j):
        for m, side, near, far, target, source in ((1, 0, H1, H2, right, left), (3, 1, H2, H1, left, right)):
            joined(j, m)
            add_into(own.at[j, m, far], [sib.at[j, m, far]], HALF)
            arrived(s1.at[j, side], s1_sems.at[j, side], source)
            add_into(own.at[j, m, near], [sib.at[j, m, near], s1.at[j, side]], HALF)
            sends.start(own.at[j, m], s2.at[j, side], s2_sems.at[j, side], target)

    def step_c(j):
        joined(j, 0)
        arrived(s2.at[j, 0], s2_sems.at[j, 0], left)
        arrived(s2.at[j, 1], s2_sems.at[j, 1], right)
        if j:
            add_into(own.at[j, 0], [sib.at[j, 0], s2.at[j, 0], s2.at[j, 1]], ROWS)
            sends.start(own.at[j, 0], zin.at[j - 1], z_sems.at[j - 1], along[j])

    a, b, c_, d = ORDER
    step_a(a)
    step_a(b)
    step_b(a)
    step_a(c_)
    step_b(b)
    step_c(a)
    step_a(d)
    step_b(c_)
    step_c(b)
    step_b(d)
    step_c(c_)
    step_c(d)
    for j in range(1, 4):
        arrived(zin.at[j - 1], z_sems.at[j - 1], along[(4 - j) % 4])

    def finish(at):
        pre = own[0, 0, at, :].astype(F32)
        for term in (sib.at[0, 0], s2.at[0, 0], s2.at[0, 1], zin.at[0], zin.at[1], zin.at[2]):
            pre = pre + term[at, :].astype(F32)
        sigma = jax.nn.sigmoid(pre)
        layer_ref[at, :] = (pre * sigma).astype(BF16)
        slope = sigma * (1.0 + pre * (1.0 - sigma))
        gown[at, :] = (cot_ref[at, :].astype(F32) * slope).astype(BF16)

    each_chunk(ROWS, 128, finish)

    def block(j, m, part=None):
        c = ((zl + 4 - j) % 4) * 8 + ((x + m) % 4) * 2 + k
        return grows_ref.at[c] if part is None else grows_ref.at[c, (H1, H2)[part]]

    def other(j, m, part=None):
        c = ((zl + 4 - j) % 4) * 8 + ((x + m) % 4) * 2 + (1 - k)
        return grows_ref.at[c] if part is None else grows_ref.at[c, (H1, H2)[part]]

    mine = pltpu.make_async_copy(gown, block(0, 0), load_sems.at[0, 0])
    mine.start()
    for j in range(1, 4):
        sends.start(gown, block(0, 0), gz_sems.at[j - 1], along[j])

    def spread(j):
        src = gown
        if j:
            src = block(j, 0)
            arrived(src, gz_sems.at[j - 1], along[(4 - j) % 4])
        sends.start(src, block(j, 0), gnear_sems.at[j, 0], right)
        sends.start(src, block(j, 0), gnear_sems.at[j, 1], left)
        sends.start(src, block(j, 0), gsib_sems.at[j, 0], sibling)

    def relay(j):
        arrived(block(j, 3), gnear_sems.at[j, 0], left)
        sends.start(block(j, 3, 0), block(j, 3, 0), gfar_sems.at[j, 0], right)
        arrived(block(j, 1), gnear_sems.at[j, 1], right)
        sends.start(block(j, 1, 1), block(j, 1, 1), gfar_sems.at[j, 1], left)
        sends.start(block(j, 3), block(j, 3), gsib_sems.at[j, 1], sibling)
        sends.start(block(j, 1), block(j, 1), gsib_sems.at[j, 2], sibling)

    def share(j):
        arrived(block(j, 2, 0), gfar_sems.at[j, 0], left)
        sends.start(block(j, 2, 0), block(j, 2, 0), gsib_sems.at[j, 3], sibling)
        arrived(block(j, 2, 1), gfar_sems.at[j, 1], right)
        sends.start(block(j, 2, 1), block(j, 2, 1), gsib_sems.at[j, 4], sibling)

    a, b, c_, d = 0, 1, 3, 2
    spread(a)
    spread(b)
    relay(a)
    spread(c_)
    relay(b)
    share(a)
    spread(d)
    relay(c_)
    share(b)
    relay(d)
    share(c_)
    share(d)
    for j in range(4):
        arrived(other(j, 0), gsib_sems.at[j, 0], sibling)
        arrived(other(j, 3), gsib_sems.at[j, 1], sibling)
        arrived(other(j, 1), gsib_sems.at[j, 2], sibling)
        arrived(other(j, 2, 0), gsib_sems.at[j, 3], sibling)
        arrived(other(j, 2, 1), gsib_sems.at[j, 4], sibling)
    sends.finish()
    mine.wait()


def middle(part, cotangent):
    vmem, anywhere = (pl.BlockSpec(memory_space=m) for m in (pltpu.VMEM, pl.ANY))
    dma = pltpu.SemaphoreType.DMA
    return pl.pallas_call(
        middle_kernel,
        out_shape=(
            jax.ShapeDtypeStruct((ROWS, 128), BF16),
            jax.ShapeDtypeStruct((32, ROWS, 128), BF16),
        ),
        in_specs=[anywhere, vmem],
        out_specs=(vmem, anywhere),
        scratch_shapes=[
            pltpu.VMEM((4, 4, ROWS, 128), BF16),
            pltpu.VMEM((4, 4, ROWS, 128), BF16),
            pltpu.VMEM((4, 2, HALF, 128), BF16),
            pltpu.VMEM((4, 2, ROWS, 128), BF16),
            pltpu.VMEM((3, ROWS, 128), BF16),
            pltpu.VMEM((ROWS, 128), BF16),
            dma((4, 4)), dma((4, 4)), dma((4, 2)), dma((4, 2)), dma((3,)), dma((80,)),
            dma((3,)), dma((4, 2)), dma((4, 2)), dma((4, 5)),
        ],
        compiler_params=pltpu.CompilerParams(
            collective_id=2, has_side_effects=True, vmem_limit_bytes=VMEM_BYTES
        ),
    )(part, cotangent)


def backward_kernel(rows_ref, cols_ref, live_ref, g_ref, tiles_ref, out_ref, gv, tiles, acc, outv, sems, g_sems):
    load_t = pltpu.make_async_copy(tiles_ref, tiles, sems.at[0])
    load_t.start()
    live = live_ref[0]

    def fetch(s):
        return pltpu.make_async_copy(g_ref.at[rows_ref[s]], gv.at[s], g_sems.at[s])

    def begin(s, carry):
        fetch(s).start()
        return carry

    lax.fori_loop(0, live, begin, 0)

    def clear(i, carry):
        acc[pl.ds(i * 2, 2)] = jnp.zeros((2, 128, 128), F32)
        return carry

    lax.fori_loop(0, 32, clear, 0)
    load_t.wait()

    def turn(i, carry):
        products = []
        for u in range(TURN):
            s = i * TURN + u
            fetch(s).wait()
        for u in range(TURN):
            s = i * TURN + u
            products.append(
                lax.dot_general(tiles[s], gv[s], (((0,), (0,)), ((), ())), preferred_element_type=F32)
            )
        for u in range(TURN):
            b = cols_ref[i * TURN + u]
            acc[b] = acc[b] + products[u]
        return carry

    lax.fori_loop(0, live // TURN, turn, 0)

    def pack(i, carry):
        outv[pl.ds(i * 2, 2)] = acc[pl.ds(i * 2, 2)].astype(BF16)
        return carry

    lax.fori_loop(0, 32, pack, 0)
    store = pltpu.make_async_copy(outv, out_ref, sems.at[1])
    store.start()
    store.wait()


def backward(rows, cols, live, grows, tiles):
    smem, anywhere = (pl.BlockSpec(memory_space=m) for m in (pltpu.SMEM, pl.ANY))
    return pl.pallas_call(
        backward_kernel,
        out_shape=jax.ShapeDtypeStruct((64, 128, 128), BF16),
        in_specs=[smem, smem, smem, anywhere, anywhere],
        out_specs=anywhere,
        scratch_shapes=[
            pltpu.VMEM((64, 128, 128), BF16),
            pltpu.VMEM((64, 128, 128), BF16),
            pltpu.VMEM((64, 128, 128), F32),
            pltpu.VMEM((64, 128, 128), BF16),
            pltpu.SemaphoreType.DMA((2,)),
            pltpu.SemaphoreType.DMA((64,)),
        ],
        compiler_params=pltpu.CompilerParams(vmem_limit_bytes=VMEM_BYTES),
    )(rows, cols, live, grows, tiles)


PIECE = ROWS // 2
QUARTER = PIECE // 2
GROW = 16


def last_kernel(
    back_ref, x_ref, w_ref, gx_ref, gw_ref,
    own, xv, s1, s2, zin, gcore, gx4, gy4, gz8, gpart, final,
    load_sems, s1_sems, s2_sems, z_sems, send_sems,
    wcore_sems, wx_sems, wy_sems, wz_sems, wg_sems, wc_sems,
):
    x, y, zh, zl, k = place()
    right, left = device(x, (y + 1) % 4, zh, zl, k), device(x, (y + 3) % 4, zh, zl, k)
    over = device(x, y, 1 - zh, zl, k)
    sibling = device(x, y, zh, zl, 1 - k)
    xs = [None] + [device((x + i) % 4, y, zh, zl, k) for i in range(1, 4)]
    ys = [None] + [device(x, (y + i) % 4, zh, zl, k) for i in range(1, 4)]
    z = zh * 4 + zl

    def at_z(v):
        return device(x, y, v // 4, v % 4, k)

    zs = [None] + [at_z((z + i) % 8) for i in range(1, 8)]
    load = pltpu.make_async_copy(back_ref, own, load_sems.at[0])
    load.start()
    load_x = pltpu.make_async_copy(x_ref, xv, load_sems.at[1])
    load_x.start()
    greet([sibling] + xs[1:] + ys[1:] + zs[1:])
    sends = Sends(send_sems)

    def dest(m, t):
        return ((y + m) % 4) * 2 + (1 - zh if t == 0 else zh)

    def rows(q, part=None):
        if part is None:
            return pl.ds(q * PIECE, PIECE)
        return pl.ds(q * PIECE + part * QUARTER, QUARTER)

    pieces = [(0, 0), (0, 1), (1, 0), (1, 1)]
    for p, (t, q) in enumerate(pieces):
        sends.start(back_ref.at[dest(2, t), rows(q, 0)], s1.at[p, 0], s1_sems.at[p, 0], right)
        sends.start(back_ref.at[dest(2, t), rows(q, 1)], s1.at[p, 1], s1_sems.at[p, 1], left)
    load.wait()
    load_x.wait()

    def step_b(p):
        t, q = pieces[p]
        for m, side, target, source in ((1, 0, right, left), (3, 1, left, right)):
            arrived(s1.at[p, side], s1_sems.at[p, side], source)
            add_into(own.at[dest(m, t), rows(q, side)], [s1.at[p, side]], QUARTER)
            sends.start(own.at[dest(m, t), rows(q)], s2.at[p, side], s2_sems.at[p, side], target)

    def step_c(p):
        t, q = pieces[p]
        arrived(s2.at[p, 0], s2_sems.at[p, 0], left)
        arrived(s2.at[p, 1], s2_sems.at[p, 1], right)
        if t == 0:
            add_into(own.at[dest(0, t), rows(q)], [s2.at[p, 0], s2.at[p, 1]], PIECE)
            sends.start(own.at[dest(0, t), rows(q)], zin.at[q], z_sems.at[q], over)

    gpart[...] = jnp.zeros((128, 128), F32)

    def weight_grad(i, carry):
        gpart[...] += lax.dot_general(
            xv[i], own[i], (((0,), (0,)), ((), ())), preferred_element_type=F32
        )
        return carry

    lax.fori_loop(0, 8, weight_grad, 0)
    sends.start(gpart.at[pl.ds((1 - k) * 64, 64)], gcore, wcore_sems.at[0], sibling)
    step_b(0)
    step_b(1)
    arrived(gcore, wcore_sems.at[0], sibling)
    mine = pl.ds(k * 64, 64)
    gpart[mine, :] = gpart[mine, :] + gcore[...]
    for i in range(1, 4):
        at = pl.ds(k * 64 + ((x + i) % 4) * GROW, GROW)
        sends.start(gpart.at[at], gx4.at[i], wx_sems.at[i], xs[i])
    step_c(0)
    for i in range(1, 4):
        arrived(gx4.at[i], wx_sems.at[i], xs[4 - i])
    share = pl.ds(k * 64 + x * GROW, GROW)
    gx4[0] = gpart[share, :] + gx4[1] + gx4[2] + gx4[3]
    for i in range(1, 4):
        sends.start(gx4.at[0], gy4.at[i], wy_sems.at[i], ys[i])
    step_b(2)
    step_c(1)
    for i in range(1, 4):
        arrived(gy4.at[i], wy_sems.at[i], ys[4 - i])
    gy4[0] = gx4[0] + gy4[1] + gy4[2] + gy4[3]
    for i in range(1, 8):
        sends.start(gy4.at[0], gz8.at[i], wz_sems.at[i], zs[i])
    step_b(3)
    for i in range(1, 8):
        arrived(gz8.at[i], wz_sems.at[i], zs[8 - i])
    total = gy4[0]
    for i in range(1, 8):
        total = total + gz8[i]
    final[share, :] = total
    for i in range(1, 4):
        sends.start(final.at[share], final.at[share], wg_sems.at[i], xs[i])
    step_c(2)
    for i in range(1, 4):
        from_x = pl.ds(k * 64 + ((x + 4 - i) % 4) * GROW, GROW)
        arrived(final.at[from_x], wg_sems.at[i], xs[4 - i])
    sends.start(final.at[mine], final.at[mine], wc_sems.at[0], sibling)
    step_c(3)
    weight = w_ref[...]
    for q in range(2):
        arrived(zin.at[q], z_sems.at[q], over)
        p = 2 + q

        def output(at):
            value = own[dest(0, 1), pl.ds(q * PIECE + at.start, at.size), :].astype(F32)
            for term in (s2.at[p, 0], s2.at[p, 1], zin.at[q]):
                value = value + term[at, :].astype(F32)
            high = value.astype(BF16)
            low = (value - high.astype(F32)).astype(BF16)
            dims = (((1,), (1,)), ((), ()))
            result = lax.dot_general(high, weight, dims, preferred_element_type=F32)
            result = result + lax.dot_general(low, weight, dims, preferred_element_type=F32)
            gx_ref[pl.ds(q * PIECE + at.start, at.size), :] = result.astype(BF16)

        each_chunk(PIECE, 256, output)
    arrived(final.at[pl.ds((1 - k) * 64, 64)], wc_sems.at[0], sibling)
    gw_ref[...] = final[...]
    sends.finish()


def last(back, x, weight):
    vmem, anywhere = (pl.BlockSpec(memory_space=m) for m in (pltpu.VMEM, pl.ANY))
    dma = pltpu.SemaphoreType.DMA
    return pl.pallas_call(
        last_kernel,
        out_shape=(jax.ShapeDtypeStruct((ROWS, 128), BF16), jax.ShapeDtypeStruct((128, 128), F32)),
        in_specs=[anywhere, anywhere, vmem],
        out_specs=(vmem, vmem),
        scratch_shapes=[
            pltpu.VMEM((8, ROWS, 128), BF16),
            pltpu.VMEM((8, ROWS, 128), BF16),
            pltpu.VMEM((4, 2, QUARTER, 128), BF16),
            pltpu.VMEM((4, 2, PIECE, 128), BF16),
            pltpu.VMEM((2, PIECE, 128), BF16),
            pltpu.VMEM((64, 128), F32),
            pltpu.VMEM((4, GROW, 128), F32),
            pltpu.VMEM((4, GROW, 128), F32),
            pltpu.VMEM((8, GROW, 128), F32),
            pltpu.VMEM((128, 128), F32),
            pltpu.VMEM((128, 128), F32),
            dma((2,)), dma((4, 2)), dma((4, 2)), dma((2,)), dma((40,)),
            dma((1,)), dma((4,)), dma((4,)), dma((8,)), dma((4,)), dma((1,)),
        ],
        compiler_params=pltpu.CompilerParams(
            collective_id=3, has_side_effects=True, vmem_limit_bytes=VMEM_BYTES
        ),
    )(back, x, weight)


def shards(features, weight, tile_values, tile_rows, tile_cols, tile_live, cotangent):
    tiles = tile_values[0, 0]
    rows = tile_rows[0, 0]
    cols = tile_cols[0, 0]
    live = tile_live[0]
    gathered = gather_row(features)
    part = forward(rows, cols, live, gathered.reshape(8 * ROWS, 128), weight, tiles)
    layer_out, grows = middle(part.reshape(32, ROWS, 128), cotangent)
    back = backward(rows, cols, live, grows.reshape(256, 128, 128), tiles)
    grad_x, grad_w = last(back.reshape(8, ROWS, 128), gathered, weight)
    return (layer_out, grad_x, grad_w)


def solution(mesh):
    in_specs = (
        P(("col", "row"), None),
        P(),
        P("row", "col", None, None, None),
        P("row", "col", None),
        P("row", "col", None),
        P("row", "col"),
        P(("row", "col"), None),
    )
    out_specs = (P(("row", "col"), None), P(("col", "row"), None), P())
    return jax.shard_map(shards, mesh=mesh, in_specs=in_specs, out_specs=out_specs, check_vma=False)
```

```python
import functools

import jax
import jax.numpy as jnp
from jax import lax
from jax.experimental import pallas as pl
from jax.experimental.pallas import tpu as pltpu
from jax.sharding import PartitionSpec as P

MESH = pl.DeviceIdType.MESH
F32 = jnp.float32
BF16 = jnp.bfloat16
ROWS = 1024
VMEM_BYTES = 56 << 20


def place():
    r, c = lax.axis_index("row"), lax.axis_index("col")
    return (c // 2) % 4, r // 2, r % 2, c // 8, c % 2


def device(x, y, zh, zl, k):
    return (y * 2 + zh, zl * 8 + x * 2 + k)


def remote(src, dst, send, recv, target):
    return pltpu.make_async_remote_copy(
        src_ref=src, dst_ref=dst, send_sem=send, recv_sem=recv, device_id=target, device_id_type=MESH
    )


def greet(partners):
    barrier = pltpu.get_barrier_semaphore()
    for partner in partners:
        pl.semaphore_signal(barrier, inc=1, device_id=partner, device_id_type=MESH)
    pl.semaphore_wait(barrier, len(partners))


class Sends:
    def __init__(self, send_sems):
        self.sems = send_sems
        self.started = []

    def start(self, src, dst, recv, target):
        copy = remote(src, dst, self.sems.at[len(self.started)], recv, target)
        copy.start()
        self.started.append(copy)

    def finish(self):
        for copy in self.started:
            copy.wait_send()


def arrived(ref, recv, me):
    remote(ref, ref, recv, recv, me).wait_recv()


def each_chunk(rows, step, body):
    def go(i, carry):
        body(pl.ds(pl.multiple_of(i * step, step), step))
        return carry

    lax.fori_loop(0, rows // step, go, 0)


def add_into(out, terms, rows, step=128):
    def body(at):
        total = out[at, :].astype(F32)
        for term in terms:
            total = total + term[at, :].astype(F32)
        out[at, :] = total.astype(out.dtype)

    each_chunk(rows, step, body)


G1 = ((0, 0, 512), (0, 512, 512), (1, 0, 256), (1, 256, 256), (1, 512, 256), (1, 768, 256))
G1_OVER = (2, 3, 4, 5)
G1_ORDER = (("far", 0), ("near", 2), ("far", 1), ("near", 3), ("far", 2), ("near", 4), ("far", 3), ("near", 5), ("far", 4), ("far", 5))


def gather_row_kernel(x_ref, out_ref, local_sem, send_sems, z_sems, near_sems, far_sems):
    x, y, zh, zl, k = place()
    right, left = device(x, (y + 1) % 4, zh, zl, k), device(x, (y + 3) % 4, zh, zl, k)
    over = device(x, y, 1 - zh, zl, k)
    greet([right, left, over])
    sends = Sends(send_sems)
    own = y * 2 + zh

    def piece(yy, p, part=None):
        side, start, size = G1[p]
        block = (yy % 4) * 2 + (1 - zh if side else zh)
        if part is not None:
            size = size // 2
            start = start + part * size
        return out_ref.at[block, pl.ds(start, size)]

    mine = pltpu.make_async_copy(x_ref, out_ref.at[own], local_sem)
    for p in G1_OVER:
        _, start, size = G1[p]
        rows = pl.ds(start, size)
        sends.start(x_ref.at[rows], out_ref.at[own, rows], z_sems.at[p], over)
    for p in (0, 1):
        _, start, size = G1[p]
        src = x_ref.at[pl.ds(start, size)]
        sends.start(src, piece(y, p), near_sems.at[p, 0], right)
        sends.start(src, piece(y, p), near_sems.at[p, 1], left)
    mine.start()

    def near(p):
        here = piece(y, p)
        arrived(here, z_sems.at[p], over)
        sends.start(here, here, near_sems.at[p, 0], right)
        sends.start(here, here, near_sems.at[p, 1], left)

    def far(p):
        arrived(piece(y + 3, p), near_sems.at[p, 0], left)
        src = piece(y + 3, p, 0)
        sends.start(src, src, far_sems.at[p, 0], right)
        arrived(piece(y + 1, p), near_sems.at[p, 1], right)
        src = piece(y + 1, p, 1)
        sends.start(src, src, far_sems.at[p, 1], left)

    for what, p in G1_ORDER:
        (near if what == "near" else far)(p)
    for p in range(len(G1)):
        arrived(piece(y + 2, p, 0), far_sems.at[p, 0], left)
        arrived(piece(y + 2, p, 1), far_sems.at[p, 1], right)
    sends.finish()
    mine.wait()


def gather_row(features):
    n = len(G1)
    return pl.pallas_call(
        gather_row_kernel,
        out_shape=jax.ShapeDtypeStruct((8, ROWS, 128), BF16),
        in_specs=[pl.BlockSpec(memory_space=pl.ANY)],
        out_specs=pl.BlockSpec(memory_space=pl.ANY),
        scratch_shapes=[
            pltpu.SemaphoreType.DMA,
            pltpu.SemaphoreType.DMA((len(G1_OVER) + 4 * n,)),
            pltpu.SemaphoreType.DMA((n,)),
            pltpu.SemaphoreType.DMA((n, 2)),
            pltpu.SemaphoreType.DMA((n, 2)),
        ],
        compiler_params=pltpu.CompilerParams(
            collective_id=1, has_side_effects=True, vmem_limit_bytes=VMEM_BYTES
        ),
    )(features)


TURN = 4


def forward_kernel(rows_ref, cols_ref, live_ref, x_ref, w_ref, tiles_ref, out_ref, xv, proj, tiles, acc, sems):
    load_x = pltpu.make_async_copy(x_ref, xv, sems.at[0])
    load_t = pltpu.make_async_copy(tiles_ref, tiles, sems.at[1])
    load_x.start()
    load_t.start()

    def clear(i, carry):
        acc[pl.ds(i * 4, 4)] = jnp.zeros((4, 128, 128), BF16)
        return carry

    lax.fori_loop(0, 64, clear, 0)
    load_x.wait()
    weight = w_ref[...]

    def project(i, carry):
        block = xv[pl.ds(pl.multiple_of(i * 512, 512), 512), :]
        value = jnp.dot(block, weight, preferred_element_type=F32).astype(BF16)
        proj[pl.ds(i * 4, 4)] = value.reshape(4, 128, 128)
        return carry

    lax.fori_loop(0, 16, project, 0)
    load_t.wait()

    def turn(i, carry):
        products = []
        for u in range(TURN):
            s = i * TURN + u
            products.append(jnp.dot(tiles[s], proj[cols_ref[s]], preferred_element_type=F32))
        for u in range(TURN):
            b = rows_ref[i * TURN + u]
            acc[b] = (acc[b].astype(F32) + products[u]).astype(BF16)
        return carry

    lax.fori_loop(0, live_ref[0] // TURN, turn, 0)
    store = pltpu.make_async_copy(acc, out_ref, sems.at[2])
    store.start()
    store.wait()


def forward(rows, cols, live, x, weight, tiles):
    smem, vmem, anywhere = (pl.BlockSpec(memory_space=m) for m in (pltpu.SMEM, pltpu.VMEM, pl.ANY))
    return pl.pallas_call(
        forward_kernel,
        out_shape=jax.ShapeDtypeStruct((256, 128, 128), BF16),
        in_specs=[smem, smem, smem, anywhere, vmem, anywhere],
        out_specs=anywhere,
        scratch_shapes=[
            pltpu.VMEM((8 * ROWS, 128), BF16),
            pltpu.VMEM((64, 128, 128), BF16),
            pltpu.VMEM((64, 128, 128), BF16),
            pltpu.VMEM((256, 128, 128), BF16),
            pltpu.SemaphoreType.DMA((3,)),
        ],
        compiler_params=pltpu.CompilerParams(vmem_limit_bytes=VMEM_BYTES),
    )(rows, cols, live, x, weight, tiles)


HALF = ROWS // 2
QUARTER = ROWS // 4
NEEDED = (
    (2, 2), (1, 2), (3, 2), (2, 1), (2, 3), (0, 2), (1, 1), (1, 3),
    (2, 0), (3, 1), (3, 3), (1, 0), (0, 1), (0, 3), (3, 0), (0, 0),
)
MIDDLE_ORDER = (
    ("a", 2, 0), ("a", 1, 0), ("a", 3, 0), ("b", 2, 0), ("a", 0, 0), ("b", 1, 0), ("a", 2, 1), ("b", 3, 0),
    ("c", 2, 0), ("a", 1, 1), ("b", 0, 0), ("c", 1, 0), ("a", 3, 1), ("b", 2, 1), ("c", 3, 0), ("a", 0, 1),
    ("b", 1, 1), ("c", 0, 0), ("end", 0, 0), ("b", 3, 1), ("c", 2, 1), ("b", 0, 1), ("near", 0, 0),
    ("c", 1, 1), ("near", 1, 0), ("c", 3, 1), ("near", 3, 0), ("c", 0, 1), ("end", 0, 1),
    ("near", 0, 1), ("far", 0, 0), ("far", 1, 0), ("near", 2, 0), ("far", 3, 0), ("near", 1, 1), ("share", 0, 0),
    ("share", 1, 0), ("far", 0, 1), ("near", 3, 1), ("far", 2, 0), ("share", 3, 0), ("far", 1, 1), ("near", 2, 1),
    ("share", 2, 0), ("share", 0, 1), ("far", 3, 1), ("share", 1, 1), ("far", 2, 1), ("share", 3, 1), ("share", 2, 1),
)


def middle_kernel(
    part_ref, cot_ref, layer_ref, grows_ref,
    own, sib, s1, s2, zin, gown,
    load_sems, sib_sems, s1_sems, s2_sems, z_sems, send_sems,
    gz_sems, gnear_sems, gfar_sems, gsib_sems, mine_sems,
):
    x, y, zh, zl, k = place()
    right, left = device((x + 1) % 4, y, zh, zl, k), device((x + 3) % 4, y, zh, zl, k)
    sibling = device(x, y, zh, zl, 1 - k)
    along = [None] + [device(x, y, zh, (zl + j) % 4, k) for j in range(1, 4)]
    halves = (pl.ds(0, HALF), pl.ds(HALF, HALF))
    loads = {}
    for j, m in NEEDED:
        c = ((zl + j) % 4) * 8 + ((x + m) % 4) * 2 + k
        loads[j, m] = pltpu.make_async_copy(part_ref.at[c], own.at[j, m], load_sems.at[j, m])
        loads[j, m].start()
    greet([right, left, sibling] + along[1:])
    sends = Sends(send_sems)
    for q in range(2):
        for j, m in NEEDED:
            c = ((zl + j) % 4) * 8 + ((x + m) % 4) * 2 + (1 - k)
            sends.start(part_ref.at[c, halves[q]], sib.at[j, m, halves[q]], sib_sems.at[j, m, q], sibling)
    loaded = set()

    def joined(j, m, q):
        if (j, m) not in loaded:
            loads[j, m].wait()
            loaded.add((j, m))
        arrived(sib.at[j, m, halves[q]], sib_sems.at[j, m, q], sibling)

    def quarters(q):
        return pl.ds(q * HALF, QUARTER), pl.ds(q * HALF + QUARTER, QUARTER)

    def step_a(j, q):
        joined(j, 2, q)
        add_into(own.at[j, 2, halves[q]], [sib.at[j, 2, halves[q]]], HALF)
        first, second = quarters(q)
        sends.start(own.at[j, 2, first], s1.at[q, j, 0], s1_sems.at[q, j, 0], right)
        sends.start(own.at[j, 2, second], s1.at[q, j, 1], s1_sems.at[q, j, 1], left)

    def step_b(j, q):
        first, second = quarters(q)
        for m, side, near, far, target, source in ((1, 0, first, second, right, left), (3, 1, second, first, left, right)):
            joined(j, m, q)
            add_into(own.at[j, m, far], [sib.at[j, m, far]], QUARTER)
            arrived(s1.at[q, j, side], s1_sems.at[q, j, side], source)
            add_into(own.at[j, m, near], [sib.at[j, m, near], s1.at[q, j, side]], QUARTER)
            sends.start(own.at[j, m, halves[q]], s2.at[q, j, side], s2_sems.at[q, j, side], target)

    def step_c(j, q):
        joined(j, 0, q)
        arrived(s2.at[q, j, 0], s2_sems.at[q, j, 0], left)
        arrived(s2.at[q, j, 1], s2_sems.at[q, j, 1], right)
        if j:
            add_into(own.at[j, 0, halves[q]], [sib.at[j, 0, halves[q]], s2.at[q, j, 0], s2.at[q, j, 1]], HALF)
            sends.start(own.at[j, 0, halves[q]], zin.at[q, j - 1], z_sems.at[q, j - 1], along[j])

    def block(j, m, q, part=None):
        c = ((zl + 4 - j) % 4) * 8 + ((x + m) % 4) * 2 + k
        return grows_ref.at[c, halves[q] if part is None else quarters(q)[part]]

    def other(j, m, q, part=None):
        c = ((zl + 4 - j) % 4) * 8 + ((x + m) % 4) * 2 + (1 - k)
        return grows_ref.at[c, halves[q] if part is None else quarters(q)[part]]

    mine = []

    def end(_, q):
        for j in range(1, 4):
            arrived(zin.at[q, j - 1], z_sems.at[q, j - 1], along[4 - j])
        base = q * HALF

        def finish(at):
            here = pl.ds(base + at.start, at.size)
            pre = own[0, 0, here, :].astype(F32) + sib[0, 0, here, :].astype(F32)
            for term in (s2.at[q, 0, 0], s2.at[q, 0, 1], zin.at[q, 0], zin.at[q, 1], zin.at[q, 2]):
                pre = pre + term[at, :].astype(F32)
            sigma = jax.nn.sigmoid(pre)
            layer_ref[here, :] = (pre * sigma).astype(BF16)
            slope = sigma * (1.0 + pre * (1.0 - sigma))
            gown[here, :] = (cot_ref[here, :].astype(F32) * slope).astype(BF16)

        each_chunk(HALF, 128, finish)
        src = gown.at[halves[q]]
        for j in (1, 3, 2):
            sends.start(src, block(0, 0, q), gz_sems.at[q, j - 1], along[j])
        mine.append(pltpu.make_async_copy(src, block(0, 0, q), mine_sems.at[q]))
        mine[-1].start()

    def near(j, q):
        src = gown.at[halves[q]]
        if j:
            src = block(j, 0, q)
            arrived(src, gz_sems.at[q, j - 1], along[4 - j])
        sends.start(src, block(j, 0, q), gnear_sems.at[q, j, 0], right)
        sends.start(src, block(j, 0, q), gnear_sems.at[q, j, 1], left)
        sends.start(src, block(j, 0, q), gsib_sems.at[q, j, 0], sibling)

    def far(j, q):
        arrived(block(j, 3, q), gnear_sems.at[q, j, 0], left)
        sends.start(block(j, 3, q, 0), block(j, 3, q, 0), gfar_sems.at[q, j, 0], right)
        arrived(block(j, 1, q), gnear_sems.at[q, j, 1], right)
        sends.start(block(j, 1, q, 1), block(j, 1, q, 1), gfar_sems.at[q, j, 1], left)
        sends.start(block(j, 3, q), block(j, 3, q), gsib_sems.at[q, j, 1], sibling)
        sends.start(block(j, 1, q), block(j, 1, q), gsib_sems.at[q, j, 2], sibling)

    def share(j, q):
        arrived(block(j, 2, q, 0), gfar_sems.at[q, j, 0], left)
        sends.start(block(j, 2, q, 0), block(j, 2, q, 0), gsib_sems.at[q, j, 3], sibling)
        arrived(block(j, 2, q, 1), gfar_sems.at[q, j, 1], right)
        sends.start(block(j, 2, q, 1), block(j, 2, q, 1), gsib_sems.at[q, j, 4], sibling)

    steps = {"a": step_a, "b": step_b, "c": step_c, "end": end, "near": near, "far": far, "share": share}
    for name, j, q in MIDDLE_ORDER:
        steps[name](j, q)
    for q in range(2):
        for j in range(4):
            arrived(other(j, 0, q), gsib_sems.at[q, j, 0], sibling)
            arrived(other(j, 3, q), gsib_sems.at[q, j, 1], sibling)
            arrived(other(j, 1, q), gsib_sems.at[q, j, 2], sibling)
            arrived(other(j, 2, q, 0), gsib_sems.at[q, j, 3], sibling)
            arrived(other(j, 2, q, 1), gsib_sems.at[q, j, 4], sibling)
    sends.finish()
    for copy in mine:
        copy.wait()


def middle(part, cotangent):
    vmem, anywhere = (pl.BlockSpec(memory_space=m) for m in (pltpu.VMEM, pl.ANY))
    dma = pltpu.SemaphoreType.DMA
    return pl.pallas_call(
        middle_kernel,
        out_shape=(
            jax.ShapeDtypeStruct((ROWS, 128), BF16),
            jax.ShapeDtypeStruct((32, ROWS, 128), BF16),
        ),
        in_specs=[anywhere, vmem],
        out_specs=(vmem, anywhere),
        scratch_shapes=[
            pltpu.VMEM((4, 4, ROWS, 128), BF16),
            pltpu.VMEM((4, 4, ROWS, 128), BF16),
            pltpu.VMEM((2, 4, 2, QUARTER, 128), BF16),
            pltpu.VMEM((2, 4, 2, HALF, 128), BF16),
            pltpu.VMEM((2, 3, HALF, 128), BF16),
            pltpu.VMEM((ROWS, 128), BF16),
            dma((4, 4)), dma((4, 4, 2)), dma((2, 4, 2)), dma((2, 4, 2)), dma((2, 3)), dma((160,)),
            dma((2, 3)), dma((2, 4, 2)), dma((2, 4, 2)), dma((2, 4, 5)), dma((2,)),
        ],
        compiler_params=pltpu.CompilerParams(
            collective_id=2, has_side_effects=True, vmem_limit_bytes=VMEM_BYTES
        ),
    )(part, cotangent)


def backward_kernel(rows_ref, cols_ref, live_ref, g_ref, tiles_ref, out_ref, gv, tiles, acc, outv, sems, g_sems):
    load_t = pltpu.make_async_copy(tiles_ref, tiles, sems.at[0])
    load_t.start()
    live = live_ref[0]

    def fetch(s):
        return pltpu.make_async_copy(g_ref.at[rows_ref[s]], gv.at[s], g_sems.at[s])

    def begin(s, carry):
        fetch(s).start()
        return carry

    lax.fori_loop(0, live, begin, 0)

    def clear(i, carry):
        acc[pl.ds(i * 2, 2)] = jnp.zeros((2, 128, 128), F32)
        return carry

    lax.fori_loop(0, 32, clear, 0)
    load_t.wait()

    def turn(i, carry):
        products = []
        for u in range(TURN):
            s = i * TURN + u
            fetch(s).wait()
        for u in range(TURN):
            s = i * TURN + u
            products.append(
                lax.dot_general(tiles[s], gv[s], (((0,), (0,)), ((), ())), preferred_element_type=F32)
            )
        for u in range(TURN):
            b = cols_ref[i * TURN + u]
            acc[b] = acc[b] + products[u]
        return carry

    lax.fori_loop(0, live // TURN, turn, 0)

    def pack(i, carry):
        outv[pl.ds(i * 2, 2)] = acc[pl.ds(i * 2, 2)].astype(BF16)
        return carry

    lax.fori_loop(0, 32, pack, 0)
    store = pltpu.make_async_copy(outv, out_ref, sems.at[1])
    store.start()
    store.wait()


def backward(rows, cols, live, grows, tiles):
    smem, anywhere = (pl.BlockSpec(memory_space=m) for m in (pltpu.SMEM, pl.ANY))
    return pl.pallas_call(
        backward_kernel,
        out_shape=jax.ShapeDtypeStruct((64, 128, 128), BF16),
        in_specs=[smem, smem, smem, anywhere, anywhere],
        out_specs=anywhere,
        scratch_shapes=[
            pltpu.VMEM((64, 128, 128), BF16),
            pltpu.VMEM((64, 128, 128), BF16),
            pltpu.VMEM((64, 128, 128), F32),
            pltpu.VMEM((64, 128, 128), BF16),
            pltpu.SemaphoreType.DMA((2,)),
            pltpu.SemaphoreType.DMA((64,)),
        ],
        compiler_params=pltpu.CompilerParams(vmem_limit_bytes=VMEM_BYTES),
    )(rows, cols, live, grows, tiles)


GROW = 16
PIECES = ((0, 0, 256), (0, 256, 256), (0, 512, 256), (0, 768, 256), (1, 0, 512), (1, 512, 512))
LAST_ORDER = (
    ("wg",), ("b", 0), ("b", 1), ("b", 2), ("b", 3), ("wx",), ("c", 0), ("wy",), ("a", 4), ("c", 1), ("a", 5),
    ("c", 2), ("c", 3), ("wz",), ("b", 4), ("b", 5), ("ws",), ("c", 4), ("wc",), ("c", 5),
)


def last_kernel(
    back_ref, x_ref, w_ref, gx_ref, gw_ref,
    own, xv, s1, s2, zin, gcore, gx4, gy4, gz8, gpart, final,
    load_sems, s1_sems, s2_sems, z_sems, send_sems,
    wcore_sems, wx_sems, wy_sems, wz_sems, wg_sems, wc_sems,
):
    x, y, zh, zl, k = place()
    right, left = device(x, (y + 1) % 4, zh, zl, k), device(x, (y + 3) % 4, zh, zl, k)
    over = device(x, y, 1 - zh, zl, k)
    sibling = device(x, y, zh, zl, 1 - k)
    xs = [None] + [device((x + i) % 4, y, zh, zl, k) for i in range(1, 4)]
    ys = [None] + [device(x, (y + i) % 4, zh, zl, k) for i in range(1, 4)]
    z = zh * 4 + zl

    def at_z(v):
        return device(x, y, v // 4, v % 4, k)

    zs = [None] + [at_z((z + i) % 8) for i in range(1, 8)]
    load = pltpu.make_async_copy(back_ref, own, load_sems.at[0])
    load.start()
    load_x = pltpu.make_async_copy(x_ref, xv, load_sems.at[1])
    load_x.start()
    greet([sibling] + xs[1:] + ys[1:] + zs[1:])
    sends = Sends(send_sems)

    def dest(m, p):
        return ((y + m) % 4) * 2 + (zh if PIECES[p][0] else 1 - zh)

    def rows(p, part=None):
        _, start, size = PIECES[p]
        if part is None:
            return pl.ds(start, size)
        return pl.ds(start + part * (size // 2), size // 2)

    def near(p, side):
        return s1.at[p, side, pl.ds(0, PIECES[p][2] // 2)]

    def far(p, side):
        return s2.at[p, side, pl.ds(0, PIECES[p][2])]

    def step_a(p):
        sends.start(back_ref.at[dest(2, p), rows(p, 0)], near(p, 0), s1_sems.at[p, 0], right)
        sends.start(back_ref.at[dest(2, p), rows(p, 1)], near(p, 1), s1_sems.at[p, 1], left)

    def step_b(p):
        for m, side, target, source in ((1, 0, right, left), (3, 1, left, right)):
            arrived(near(p, side), s1_sems.at[p, side], source)
            add_into(own.at[dest(m, p), rows(p, side)], [near(p, side)], PIECES[p][2] // 2)
            sends.start(own.at[dest(m, p), rows(p)], far(p, side), s2_sems.at[p, side], target)

    def step_c(p):
        arrived(far(p, 0), s2_sems.at[p, 0], left)
        arrived(far(p, 1), s2_sems.at[p, 1], right)
        if PIECES[p][0] == 0:
            add_into(own.at[dest(0, p), rows(p)], [far(p, 0), far(p, 1)], PIECES[p][2])
            sends.start(own.at[dest(0, p), rows(p)], zin.at[rows(p)], z_sems.at[p], over)

    mine = pl.ds(k * 64, 64)
    theirs = pl.ds((1 - k) * 64, 64)
    share = pl.ds(k * 64 + x * GROW, GROW)

    def weight_grad():
        load.wait()
        load_x.wait()
        gpart[...] = jnp.zeros((128, 128), F32)

        def block(i, carry):
            gpart[...] += lax.dot_general(
                xv[i], own[i], (((0,), (0,)), ((), ())), preferred_element_type=F32
            )
            return carry

        lax.fori_loop(0, 8, block, 0)
        sends.start(gpart.at[theirs], gcore, wcore_sems.at[0], sibling)

    def weight_x():
        arrived(gcore, wcore_sems.at[0], sibling)
        gpart[mine, :] = gpart[mine, :] + gcore[...]
        for i in range(1, 4):
            at = pl.ds(k * 64 + ((x + i) % 4) * GROW, GROW)
            sends.start(gpart.at[at], gx4.at[i], wx_sems.at[i], xs[i])

    def weight_y():
        for i in range(1, 4):
            arrived(gx4.at[i], wx_sems.at[i], xs[4 - i])
        gx4[0] = gpart[share, :] + gx4[1] + gx4[2] + gx4[3]
        for i in range(1, 4):
            sends.start(gx4.at[0], gy4.at[i], wy_sems.at[i], ys[i])

    def weight_z():
        for i in range(1, 4):
            arrived(gy4.at[i], wy_sems.at[i], ys[4 - i])
        gy4[0] = gx4[0] + gy4[1] + gy4[2] + gy4[3]
        for i in range(1, 8):
            sends.start(gy4.at[0], gz8.at[i], wz_sems.at[i], zs[i])

    def weight_share():
        for i in range(1, 8):
            arrived(gz8.at[i], wz_sems.at[i], zs[8 - i])
        total = gy4[0]
        for i in range(1, 8):
            total = total + gz8[i]
        final[share, :] = total
        for i in range(1, 4):
            sends.start(final.at[share], final.at[share], wg_sems.at[i], xs[i])

    def weight_core():
        for i in range(1, 4):
            from_x = pl.ds(k * 64 + ((x + 4 - i) % 4) * GROW, GROW)
            arrived(final.at[from_x], wg_sems.at[i], xs[4 - i])
        sends.start(final.at[mine], final.at[mine], wc_sems.at[0], sibling)

    for p in range(4):
        step_a(p)
    steps = {
        "a": step_a, "b": step_b, "c": step_c, "wg": weight_grad, "wx": weight_x, "wy": weight_y,
        "wz": weight_z, "ws": weight_share, "wc": weight_core,
    }
    for name, *which in LAST_ORDER:
        steps[name](*which)
    weight = w_ref[...]
    for p in range(4):
        arrived(zin.at[rows(p)], z_sems.at[p], over)
    for p in (4, 5):
        start = PIECES[p][1]

        def output(at):
            here = pl.ds(start + at.start, at.size)
            value = own[dest(0, p), here, :].astype(F32) + zin[here, :].astype(F32)
            for term in (far(p, 0), far(p, 1)):
                value = value + term[at, :].astype(F32)
            high = value.astype(BF16)
            low = (value - high.astype(F32)).astype(BF16)
            dims = (((1,), (1,)), ((), ()))
            result = lax.dot_general(high, weight, dims, preferred_element_type=F32)
            result = result + lax.dot_general(low, weight, dims, preferred_element_type=F32)
            gx_ref[here, :] = result.astype(BF16)

        each_chunk(PIECES[p][2], 256, output)
    arrived(final.at[theirs], wc_sems.at[0], sibling)
    gw_ref[...] = final[...]
    sends.finish()


def last(back, x, weight):
    vmem, anywhere = (pl.BlockSpec(memory_space=m) for m in (pltpu.VMEM, pl.ANY))
    dma = pltpu.SemaphoreType.DMA
    n = len(PIECES)
    return pl.pallas_call(
        last_kernel,
        out_shape=(jax.ShapeDtypeStruct((ROWS, 128), BF16), jax.ShapeDtypeStruct((128, 128), F32)),
        in_specs=[anywhere, anywhere, vmem],
        out_specs=(vmem, vmem),
        scratch_shapes=[
            pltpu.VMEM((8, ROWS, 128), BF16),
            pltpu.VMEM((8, ROWS, 128), BF16),
            pltpu.VMEM((n, 2, 256, 128), BF16),
            pltpu.VMEM((n, 2, 512, 128), BF16),
            pltpu.VMEM((ROWS, 128), BF16),
            pltpu.VMEM((64, 128), F32),
            pltpu.VMEM((4, GROW, 128), F32),
            pltpu.VMEM((4, GROW, 128), F32),
            pltpu.VMEM((8, GROW, 128), F32),
            pltpu.VMEM((128, 128), F32),
            pltpu.VMEM((128, 128), F32),
            dma((2,)), dma((n, 2)), dma((n, 2)), dma((n,)), dma((48,)),
            dma((1,)), dma((4,)), dma((4,)), dma((8,)), dma((4,)), dma((1,)),
        ],
        compiler_params=pltpu.CompilerParams(
            collective_id=3, has_side_effects=True, vmem_limit_bytes=VMEM_BYTES
        ),
    )(back, x, weight)


def shards(features, weight, tile_values, tile_rows, tile_cols, tile_live, cotangent):
    tiles = tile_values[0, 0]
    rows = tile_rows[0, 0]
    cols = tile_cols[0, 0]
    live = tile_live[0]
    gathered = gather_row(features)
    part = forward(rows, cols, live, gathered.reshape(8 * ROWS, 128), weight, tiles)
    layer_out, grows = middle(part.reshape(32, ROWS, 128), cotangent)
    back = backward(rows, cols, live, grows.reshape(256, 128, 128), tiles)
    grad_x, grad_w = last(back.reshape(8, ROWS, 128), gathered, weight)
    return (layer_out, grad_x, grad_w)


def solution(mesh):
    in_specs = (
        P(("col", "row"), None),
        P(),
        P("row", "col", None, None, None),
        P("row", "col", None),
        P("row", "col", None),
        P("row", "col"),
        P(("row", "col"), None),
    )
    out_specs = (P(("row", "col"), None), P(("col", "row"), None), P())
    return jax.shard_map(shards, mesh=mesh, in_specs=in_specs, out_specs=out_specs, check_vma=False)
```

```python
import functools

import jax
import jax.numpy as jnp
from jax import lax
from jax.experimental import pallas as pl
from jax.experimental.pallas import tpu as pltpu
from jax.sharding import PartitionSpec as P

MESH = pl.DeviceIdType.MESH
F32 = jnp.float32
BF16 = jnp.bfloat16
ROWS = 1024
VMEM_BYTES = 56 << 20


def place():
    r, c = lax.axis_index("row"), lax.axis_index("col")
    return (c // 2) % 4, r // 2, r % 2, c // 8, c % 2


def device(x, y, zh, zl, k):
    return (y * 2 + zh, zl * 8 + x * 2 + k)


def remote(src, dst, send, recv, target):
    return pltpu.make_async_remote_copy(
        src_ref=src, dst_ref=dst, send_sem=send, recv_sem=recv, device_id=target, device_id_type=MESH
    )


def greet(partners):
    barrier = pltpu.get_barrier_semaphore()
    for partner in partners:
        pl.semaphore_signal(barrier, inc=1, device_id=partner, device_id_type=MESH)
    pl.semaphore_wait(barrier, len(partners))


class Sends:
    def __init__(self, send_sems):
        self.sems = send_sems
        self.started = []

    def start(self, src, dst, recv, target):
        copy = remote(src, dst, self.sems.at[len(self.started)], recv, target)
        copy.start()
        self.started.append(copy)

    def finish(self):
        for copy in self.started:
            copy.wait_send()


def arrived(ref, recv, me):
    remote(ref, ref, recv, recv, me).wait_recv()


def each_chunk(rows, step, body):
    def go(i, carry):
        body(pl.ds(pl.multiple_of(i * step, step), step))
        return carry

    lax.fori_loop(0, rows // step, go, 0)


def add_into(out, terms, rows, step=128):
    def body(at):
        total = out[at, :].astype(F32)
        for term in terms:
            total = total + term[at, :].astype(F32)
        out[at, :] = total.astype(out.dtype)

    each_chunk(rows, step, body)


G1 = ((0, 0, 512), (0, 512, 512), (1, 0, 256), (1, 256, 256), (1, 512, 256), (1, 768, 256))
G1_OVER = (2, 3, 4, 5)
G1_ORDER = (("far", 0), ("near", 2), ("far", 1), ("near", 3), ("far", 2), ("near", 4), ("far", 3), ("near", 5), ("far", 4), ("far", 5))


def slot_table(rows, cols, live):
    slots = rows.shape[1]
    i = lax.broadcasted_iota(jnp.int32, (slots, slots), 0)
    lane = lax.broadcasted_iota(jnp.int32, (slots, slots), 1)

    def upright(v):
        return jnp.sum(jnp.where(i == lane, v, 0.0), axis=1, keepdims=True)

    owner = jnp.floor(rows * 0.125)
    owner_up, rows_up, cols_up = upright(owner), upright(rows), upright(cols)
    earlier = jnp.where((owner_up == owner) & (lane < i), 1.0, 0.0)
    rank = jnp.sum(earlier, axis=1, keepdims=True)
    slot = lax.broadcasted_iota(jnp.int32, (slots, 128), 0)
    entry = lax.broadcasted_iota(jnp.int32, (slots, 128), 1).astype(F32)
    chosen = jnp.where((owner_up * 4.0 + rank == entry) & (slot < live), 1.0, 0.0)

    def pick(v):
        return jnp.sum(chosen * v, axis=0, keepdims=True)

    return pick(slot.astype(F32) - 64.0) + 64.0, pick(rows_up - owner_up * 8.0), pick(cols_up)


def gather_row_kernel(
    live_ref, x_ref, rows_ref, cols_ref, out_ref, table_ref, local_sem, send_sems, z_sems, near_sems, far_sems
):
    x, y, zh, zl, k = place()
    right, left = device(x, (y + 1) % 4, zh, zl, k), device(x, (y + 3) % 4, zh, zl, k)
    over = device(x, y, 1 - zh, zl, k)
    greet([right, left, over])
    sends = Sends(send_sems)
    own = y * 2 + zh

    def piece(yy, p, part=None):
        side, start, size = G1[p]
        block = (yy % 4) * 2 + (1 - zh if side else zh)
        if part is not None:
            size = size // 2
            start = start + part * size
        return out_ref.at[block, pl.ds(start, size)]

    mine = pltpu.make_async_copy(x_ref, out_ref.at[own], local_sem)
    for p in G1_OVER:
        _, start, size = G1[p]
        rows = pl.ds(start, size)
        sends.start(x_ref.at[rows], out_ref.at[own, rows], z_sems.at[p], over)
    for p in (0, 1):
        _, start, size = G1[p]
        src = x_ref.at[pl.ds(start, size)]
        sends.start(src, piece(y, p), near_sems.at[p, 0], right)
        sends.start(src, piece(y, p), near_sems.at[p, 1], left)
    mine.start()

    def near(p):
        here = piece(y, p)
        arrived(here, z_sems.at[p], over)
        sends.start(here, here, near_sems.at[p, 0], right)
        sends.start(here, here, near_sems.at[p, 1], left)

    def far(p):
        arrived(piece(y + 3, p), near_sems.at[p, 0], left)
        src = piece(y + 3, p, 0)
        sends.start(src, src, far_sems.at[p, 0], right)
        arrived(piece(y + 1, p), near_sems.at[p, 1], right)
        src = piece(y + 1, p, 1)
        sends.start(src, src, far_sems.at[p, 1], left)

    table_ref[...] = jnp.zeros((8, 128), jnp.int32)
    values = slot_table(rows_ref[...].astype(F32), cols_ref[...].astype(F32), live_ref[0])
    for n, value in enumerate(values):
        table_ref[n : n + 1, :] = value.astype(jnp.int32)
    for what, p in G1_ORDER:
        (near if what == "near" else far)(p)
    for p in range(len(G1)):
        arrived(piece(y + 2, p, 0), far_sems.at[p, 0], left)
        arrived(piece(y + 2, p, 1), far_sems.at[p, 1], right)
    sends.finish()
    mine.wait()


def gather_row(features, rows, cols, live):
    n = len(G1)
    smem, vmem, anywhere = (pl.BlockSpec(memory_space=m) for m in (pltpu.SMEM, pltpu.VMEM, pl.ANY))
    return pl.pallas_call(
        gather_row_kernel,
        out_shape=(
            jax.ShapeDtypeStruct((8, ROWS, 128), BF16),
            jax.ShapeDtypeStruct((8, 128), jnp.int32),
        ),
        in_specs=[smem, anywhere, vmem, vmem],
        out_specs=(anywhere, vmem),
        scratch_shapes=[
            pltpu.SemaphoreType.DMA,
            pltpu.SemaphoreType.DMA((len(G1_OVER) + 4 * n,)),
            pltpu.SemaphoreType.DMA((n,)),
            pltpu.SemaphoreType.DMA((n, 2)),
            pltpu.SemaphoreType.DMA((n, 2)),
        ],
        compiler_params=pltpu.CompilerParams(
            collective_id=1, has_side_effects=True, vmem_limit_bytes=VMEM_BYTES
        ),
    )(live, features, rows, cols)


HALF = ROWS // 2
QUARTER = ROWS // 4
NEEDED = (
    (2, 2), (1, 2), (3, 2), (2, 1), (2, 3), (0, 2), (1, 1), (1, 3),
    (2, 0), (3, 1), (3, 3), (1, 0), (0, 1), (0, 3), (3, 0), (0, 0),
)
AHEAD = 2
MIDDLE_ORDER = (
    ("a", 2, 0), ("a", 1, 0), ("a", 3, 0), ("b", 2, 0), ("a", 0, 0), ("b", 1, 0), ("a", 2, 1), ("b", 3, 0),
    ("c", 2, 0), ("a", 1, 1), ("b", 0, 0), ("c", 1, 0), ("a", 3, 1), ("b", 2, 1), ("c", 3, 0), ("a", 0, 1),
    ("b", 1, 1), ("c", 0, 0), ("end", 0, 0), ("b", 3, 1), ("c", 2, 1), ("b", 0, 1), ("near", 0, 0),
    ("c", 1, 1), ("near", 1, 0), ("c", 3, 1), ("near", 3, 0), ("c", 0, 1), ("end", 0, 1),
    ("near", 0, 1), ("far", 0, 0), ("far", 1, 0), ("near", 2, 0), ("far", 3, 0), ("near", 1, 1), ("share", 0, 0),
    ("share", 1, 0), ("far", 0, 1), ("near", 3, 1), ("far", 2, 0), ("share", 3, 0), ("far", 1, 1), ("near", 2, 1),
    ("share", 2, 0), ("share", 0, 1), ("far", 3, 1), ("share", 1, 1), ("far", 2, 1), ("share", 3, 1), ("share", 2, 1),
)


def middle_kernel(
    table_ref, x_ref, w_ref, tiles_ref, cot_ref, layer_ref, grows_ref,
    xv, proj, tiles, products, both, sib, s1, s2, zin, gown,
    load_sems, sib_sems, s1_sems, s2_sems, z_sems, send_sems,
    gz_sems, gnear_sems, gfar_sems, gsib_sems, mine_sems,
):
    x, y, zh, zl, k = place()
    right, left = device((x + 1) % 4, y, zh, zl, k), device((x + 3) % 4, y, zh, zl, k)
    sibling = device(x, y, zh, zl, 1 - k)
    along = [None] + [device(x, y, zh, (zl + j) % 4, k) for j in range(1, 4)]
    halves = (pl.ds(0, HALF), pl.ds(HALF, HALF))
    own = both.at[1]
    load_x = pltpu.make_async_copy(x_ref, xv, load_sems.at[0])
    load_x.start()
    load_t = pltpu.make_async_copy(tiles_ref, tiles.at[pl.ds(0, 64)], load_sems.at[1])
    load_t.start()
    tiles[64] = jnp.zeros((128, 128), BF16)
    load_x.wait()

    def project(i, carry):
        rows = xv[pl.ds(pl.multiple_of(i * 512, 512), 512), :]
        value = jnp.dot(rows, w_ref[...], preferred_element_type=F32).astype(BF16)
        proj[pl.ds(i * 4, 4)] = value.reshape(4, 128, 128)
        return carry

    lax.fori_loop(0, 16, project, 0)
    load_t.wait()
    greet([right, left, sibling] + along[1:])
    sends = Sends(send_sems)

    def produce(j, m):
        def side(i, carry):
            core = (1 - k) + i * (2 * k - 1)
            entry = (((zl + j) % 4) * 8 + ((x + m) % 4) * 2 + core) * 4
            for n in range(4):
                products[n] = jnp.dot(
                    tiles[table_ref[0, entry + n]], proj[table_ref[2, entry + n]], preferred_element_type=F32
                )

            def place_block(b, inner):
                total = jnp.zeros((128, 128), F32)
                for n in range(4):
                    total = total + jnp.where(table_ref[1, entry + n] == b, products[n], 0.0)
                both[i, j, m, pl.ds(pl.multiple_of(b * 128, 128), 128), :] = total.astype(BF16)
                return inner

            lax.fori_loop(0, 8, place_block, 0)
            return carry

        lax.fori_loop(0, 2, side, 0)
        for q in range(2):
            sends.start(both.at[0, j, m, halves[q]], sib.at[j, m, halves[q]], sib_sems.at[j, m, q], sibling)

    produced = []

    def joined(j, m, q):
        while len(produced) < len(NEEDED) and len(produced) <= NEEDED.index((j, m)) + AHEAD:
            produce(*NEEDED[len(produced)])
            produced.append(True)
        arrived(sib.at[j, m, halves[q]], sib_sems.at[j, m, q], sibling)

    def quarters(q):
        return pl.ds(q * HALF, QUARTER), pl.ds(q * HALF + QUARTER, QUARTER)

    def step_a(j, q):
        joined(j, 2, q)
        add_into(own.at[j, 2, halves[q]], [sib.at[j, 2, halves[q]]], HALF)
        first, second = quarters(q)
        sends.start(own.at[j, 2, first], s1.at[q, j, 0], s1_sems.at[q, j, 0], right)
        sends.start(own.at[j, 2, second], s1.at[q, j, 1], s1_sems.at[q, j, 1], left)

    def step_b(j, q):
        first, second = quarters(q)
        for m, side, near, far, target, source in ((1, 0, first, second, right, left), (3, 1, second, first, left, right)):
            joined(j, m, q)
            add_into(own.at[j, m, far], [sib.at[j, m, far]], QUARTER)
            arrived(s1.at[q, j, side], s1_sems.at[q, j, side], source)
            add_into(own.at[j, m, near], [sib.at[j, m, near], s1.at[q, j, side]], QUARTER)
            sends.start(own.at[j, m, halves[q]], s2.at[q, j, side], s2_sems.at[q, j, side], target)

    def step_c(j, q):
        joined(j, 0, q)
        arrived(s2.at[q, j, 0], s2_sems.at[q, j, 0], left)
        arrived(s2.at[q, j, 1], s2_sems.at[q, j, 1], right)
        if j:
            add_into(own.at[j, 0, halves[q]], [sib.at[j, 0, halves[q]], s2.at[q, j, 0], s2.at[q, j, 1]], HALF)
            sends.start(own.at[j, 0, halves[q]], zin.at[q, j - 1], z_sems.at[q, j - 1], along[j])

    def block(j, m, q, part=None):
        c = ((zl + 4 - j) % 4) * 8 + ((x + m) % 4) * 2 + k
        return grows_ref.at[c, halves[q] if part is None else quarters(q)[part]]

    def other(j, m, q, part=None):
        c = ((zl + 4 - j) % 4) * 8 + ((x + m) % 4) * 2 + (1 - k)
        return grows_ref.at[c, halves[q] if part is None else quarters(q)[part]]

    mine = []

    def end(_, q):
        for j in range(1, 4):
            arrived(zin.at[q, j - 1], z_sems.at[q, j - 1], along[4 - j])
        base = q * HALF

        def finish(at):
            here = pl.ds(base + at.start, at.size)
            pre = own[0, 0, here, :].astype(F32) + sib[0, 0, here, :].astype(F32)
            for term in (s2.at[q, 0, 0], s2.at[q, 0, 1], zin.at[q, 0], zin.at[q, 1], zin.at[q, 2]):
                pre = pre + term[at, :].astype(F32)
            sigma = jax.nn.sigmoid(pre)
            layer_ref[here, :] = (pre * sigma).astype(BF16)
            slope = sigma * (1.0 + pre * (1.0 - sigma))
            gown[here, :] = (cot_ref[here, :].astype(F32) * slope).astype(BF16)

        each_chunk(HALF, 128, finish)
        src = gown.at[halves[q]]
        for j in (1, 3, 2):
            sends.start(src, block(0, 0, q), gz_sems.at[q, j - 1], along[j])
        mine.append(pltpu.make_async_copy(src, block(0, 0, q), mine_sems.at[q]))
        mine[-1].start()

    def near(j, q):
        src = gown.at[halves[q]]
        if j:
            src = block(j, 0, q)
            arrived(src, gz_sems.at[q, j - 1], along[4 - j])
        sends.start(src, block(j, 0, q), gnear_sems.at[q, j, 0], right)
        sends.start(src, block(j, 0, q), gnear_sems.at[q, j, 1], left)
        sends.start(src, block(j, 0, q), gsib_sems.at[q, j, 0], sibling)

    def far(j, q):
        arrived(block(j, 3, q), gnear_sems.at[q, j, 0], left)
        sends.start(block(j, 3, q, 0), block(j, 3, q, 0), gfar_sems.at[q, j, 0], right)
        arrived(block(j, 1, q), gnear_sems.at[q, j, 1], right)
        sends.start(block(j, 1, q, 1), block(j, 1, q, 1), gfar_sems.at[q, j, 1], left)
        sends.start(block(j, 3, q), block(j, 3, q), gsib_sems.at[q, j, 1], sibling)
        sends.start(block(j, 1, q), block(j, 1, q), gsib_sems.at[q, j, 2], sibling)

    def share(j, q):
        arrived(block(j, 2, q, 0), gfar_sems.at[q, j, 0], left)
        sends.start(block(j, 2, q, 0), block(j, 2, q, 0), gsib_sems.at[q, j, 3], sibling)
        arrived(block(j, 2, q, 1), gfar_sems.at[q, j, 1], right)
        sends.start(block(j, 2, q, 1), block(j, 2, q, 1), gsib_sems.at[q, j, 4], sibling)

    steps = {"a": step_a, "b": step_b, "c": step_c, "end": end, "near": near, "far": far, "share": share}
    for name, j, q in MIDDLE_ORDER:
        steps[name](j, q)
    for q in range(2):
        for j in range(4):
            arrived(other(j, 0, q), gsib_sems.at[q, j, 0], sibling)
            arrived(other(j, 3, q), gsib_sems.at[q, j, 1], sibling)
            arrived(other(j, 1, q), gsib_sems.at[q, j, 2], sibling)
            arrived(other(j, 2, q, 0), gsib_sems.at[q, j, 3], sibling)
            arrived(other(j, 2, q, 1), gsib_sems.at[q, j, 4], sibling)
    sends.finish()
    for copy in mine:
        copy.wait()


def middle(table, x, weight, tiles, cotangent):
    smem, vmem, anywhere = (pl.BlockSpec(memory_space=m) for m in (pltpu.SMEM, pltpu.VMEM, pl.ANY))
    dma = pltpu.SemaphoreType.DMA
    return pl.pallas_call(
        middle_kernel,
        out_shape=(
            jax.ShapeDtypeStruct((ROWS, 128), BF16),
            jax.ShapeDtypeStruct((32, ROWS, 128), BF16),
        ),
        in_specs=[smem, anywhere, vmem, anywhere, vmem],
        out_specs=(vmem, anywhere),
        scratch_shapes=[
            pltpu.VMEM((8 * ROWS, 128), BF16),
            pltpu.VMEM((64, 128, 128), BF16),
            pltpu.VMEM((65, 128, 128), BF16),
            pltpu.VMEM((4, 128, 128), F32),
            pltpu.VMEM((2, 4, 4, ROWS, 128), BF16),
            pltpu.VMEM((4, 4, ROWS, 128), BF16),
            pltpu.VMEM((2, 4, 2, QUARTER, 128), BF16),
            pltpu.VMEM((2, 4, 2, HALF, 128), BF16),
            pltpu.VMEM((2, 3, HALF, 128), BF16),
            pltpu.VMEM((ROWS, 128), BF16),
            dma((2,)), dma((4, 4, 2)), dma((2, 4, 2)), dma((2, 4, 2)), dma((2, 3)), dma((160,)),
            dma((2, 3)), dma((2, 4, 2)), dma((2, 4, 2)), dma((2, 4, 5)), dma((2,)),
        ],
        compiler_params=pltpu.CompilerParams(
            collective_id=2, has_side_effects=True, vmem_limit_bytes=VMEM_BYTES
        ),
    )(table, x, weight, tiles, cotangent)


TURN = 4


def backward_kernel(rows_ref, cols_ref, live_ref, g_ref, tiles_ref, out_ref, gv, tiles, acc, outv, sems, g_sems):
    load_t = pltpu.make_async_copy(tiles_ref, tiles, sems.at[0])
    load_t.start()
    live = live_ref[0]

    def fetch(s):
        return pltpu.make_async_copy(g_ref.at[rows_ref[s]], gv.at[s], g_sems.at[s])

    def begin(s, carry):
        fetch(s).start()
        return carry

    lax.fori_loop(0, live, begin, 0)

    def clear(i, carry):
        acc[pl.ds(i * 2, 2)] = jnp.zeros((2, 128, 128), F32)
        return carry

    lax.fori_loop(0, 32, clear, 0)
    load_t.wait()

    def turn(i, carry):
        products = []
        for u in range(TURN):
            s = i * TURN + u
            fetch(s).wait()
        for u in range(TURN):
            s = i * TURN + u
            products.append(
                lax.dot_general(tiles[s], gv[s], (((0,), (0,)), ((), ())), preferred_element_type=F32)
            )
        for u in range(TURN):
            b = cols_ref[i * TURN + u]
            acc[b] = acc[b] + products[u]
        return carry

    lax.fori_loop(0, live // TURN, turn, 0)

    def pack(i, carry):
        outv[pl.ds(i * 2, 2)] = acc[pl.ds(i * 2, 2)].astype(BF16)
        return carry

    lax.fori_loop(0, 32, pack, 0)
    store = pltpu.make_async_copy(outv, out_ref, sems.at[1])
    store.start()
    store.wait()


def backward(rows, cols, live, grows, tiles):
    smem, anywhere = (pl.BlockSpec(memory_space=m) for m in (pltpu.SMEM, pl.ANY))
    return pl.pallas_call(
        backward_kernel,
        out_shape=jax.ShapeDtypeStruct((64, 128, 128), BF16),
        in_specs=[smem, smem, smem, anywhere, anywhere],
        out_specs=anywhere,
        scratch_shapes=[
            pltpu.VMEM((64, 128, 128), BF16),
            pltpu.VMEM((64, 128, 128), BF16),
            pltpu.VMEM((64, 128, 128), F32),
            pltpu.VMEM((64, 128, 128), BF16),
            pltpu.SemaphoreType.DMA((2,)),
            pltpu.SemaphoreType.DMA((64,)),
        ],
        compiler_params=pltpu.CompilerParams(vmem_limit_bytes=VMEM_BYTES),
    )(rows, cols, live, grows, tiles)


GROW = 16
PIECES = ((0, 0, 256), (0, 256, 256), (0, 512, 256), (0, 768, 256), (1, 0, 512), (1, 512, 512))
LAST_ORDER = (
    ("wg",), ("b", 0), ("b", 1), ("b", 2), ("b", 3), ("wx",), ("c", 0), ("wy",), ("a", 4), ("c", 1), ("a", 5),
    ("c", 2), ("c", 3), ("wz",), ("b", 4), ("b", 5), ("ws",), ("c", 4), ("wc",), ("c", 5),
)


def last_kernel(
    back_ref, x_ref, w_ref, gx_ref, gw_ref,
    own, xv, s1, s2, zin, gcore, gx4, gy4, gz8, gpart, final,
    load_sems, s1_sems, s2_sems, z_sems, send_sems,
    wcore_sems, wx_sems, wy_sems, wz_sems, wg_sems, wc_sems,
):
    x, y, zh, zl, k = place()
    right, left = device(x, (y + 1) % 4, zh, zl, k), device(x, (y + 3) % 4, zh, zl, k)
    over = device(x, y, 1 - zh, zl, k)
    sibling = device(x, y, zh, zl, 1 - k)
    xs = [None] + [device((x + i) % 4, y, zh, zl, k) for i in range(1, 4)]
    ys = [None] + [device(x, (y + i) % 4, zh, zl, k) for i in range(1, 4)]
    z = zh * 4 + zl

    def at_z(v):
        return device(x, y, v // 4, v % 4, k)

    zs = [None] + [at_z((z + i) % 8) for i in range(1, 8)]
    load = pltpu.make_async_copy(back_ref, own, load_sems.at[0])
    load.start()
    load_x = pltpu.make_async_copy(x_ref, xv, load_sems.at[1])
    load_x.start()
    greet([sibling] + xs[1:] + ys[1:] + zs[1:])
    sends = Sends(send_sems)

    def dest(m, p):
        return ((y + m) % 4) * 2 + (zh if PIECES[p][0] else 1 - zh)

    def rows(p, part=None):
        _, start, size = PIECES[p]
        if part is None:
            return pl.ds(start, size)
        return pl.ds(start + part * (size // 2), size // 2)

    def near(p, side):
        return s1.at[p, side, pl.ds(0, PIECES[p][2] // 2)]

    def far(p, side):
        return s2.at[p, side, pl.ds(0, PIECES[p][2])]

    def step_a(p):
        sends.start(back_ref.at[dest(2, p), rows(p, 0)], near(p, 0), s1_sems.at[p, 0], right)
        sends.start(back_ref.at[dest(2, p), rows(p, 1)], near(p, 1), s1_sems.at[p, 1], left)

    def step_b(p):
        for m, side, target, source in ((1, 0, right, left), (3, 1, left, right)):
            arrived(near(p, side), s1_sems.at[p, side], source)
            add_into(own.at[dest(m, p), rows(p, side)], [near(p, side)], PIECES[p][2] // 2)
            sends.start(own.at[dest(m, p), rows(p)], far(p, side), s2_sems.at[p, side], target)

    def step_c(p):
        arrived(far(p, 0), s2_sems.at[p, 0], left)
        arrived(far(p, 1), s2_sems.at[p, 1], right)
        if PIECES[p][0] == 0:
            add_into(own.at[dest(0, p), rows(p)], [far(p, 0), far(p, 1)], PIECES[p][2])
            sends.start(own.at[dest(0, p), rows(p)], zin.at[rows(p)], z_sems.at[p], over)

    mine = pl.ds(k * 64, 64)
    theirs = pl.ds((1 - k) * 64, 64)
    share = pl.ds(k * 64 + x * GROW, GROW)

    def weight_grad():
        load.wait()
        load_x.wait()
        gpart[...] = jnp.zeros((128, 128), F32)

        def block(i, carry):
            gpart[...] += lax.dot_general(
                xv[i], own[i], (((0,), (0,)), ((), ())), preferred_element_type=F32
            )
            return carry

        lax.fori_loop(0, 8, block, 0)
        sends.start(gpart.at[theirs], gcore, wcore_sems.at[0], sibling)

    def weight_x():
        arrived(gcore, wcore_sems.at[0], sibling)
        gpart[mine, :] = gpart[mine, :] + gcore[...]
        for i in range(1, 4):
            at = pl.ds(k * 64 + ((x + i) % 4) * GROW, GROW)
            sends.start(gpart.at[at], gx4.at[i], wx_sems.at[i], xs[i])

    def weight_y():
        for i in range(1, 4):
            arrived(gx4.at[i], wx_sems.at[i], xs[4 - i])
        gx4[0] = gpart[share, :] + gx4[1] + gx4[2] + gx4[3]
        for i in range(1, 4):
            sends.start(gx4.at[0], gy4.at[i], wy_sems.at[i], ys[i])

    def weight_z():
        for i in range(1, 4):
            arrived(gy4.at[i], wy_sems.at[i], ys[4 - i])
        gy4[0] = gx4[0] + gy4[1] + gy4[2] + gy4[3]
        for i in range(1, 8):
            sends.start(gy4.at[0], gz8.at[i], wz_sems.at[i], zs[i])

    def weight_share():
        for i in range(1, 8):
            arrived(gz8.at[i], wz_sems.at[i], zs[8 - i])
        total = gy4[0]
        for i in range(1, 8):
            total = total + gz8[i]
        final[share, :] = total
        for i in range(1, 4):
            sends.start(final.at[share], final.at[share], wg_sems.at[i], xs[i])

    def weight_core():
        for i in range(1, 4):
            from_x = pl.ds(k * 64 + ((x + 4 - i) % 4) * GROW, GROW)
            arrived(final.at[from_x], wg_sems.at[i], xs[4 - i])
        sends.start(final.at[mine], final.at[mine], wc_sems.at[0], sibling)

    for p in range(4):
        step_a(p)
    steps = {
        "a": step_a, "b": step_b, "c": step_c, "wg": weight_grad, "wx": weight_x, "wy": weight_y,
        "wz": weight_z, "ws": weight_share, "wc": weight_core,
    }
    for name, *which in LAST_ORDER:
        steps[name](*which)
    weight = w_ref[...]
    for p in range(4):
        arrived(zin.at[rows(p)], z_sems.at[p], over)
    for p in (4, 5):
        start = PIECES[p][1]

        def output(at):
            here = pl.ds(start + at.start, at.size)
            value = own[dest(0, p), here, :].astype(F32) + zin[here, :].astype(F32)
            for term in (far(p, 0), far(p, 1)):
                value = value + term[at, :].astype(F32)
            high = value.astype(BF16)
            low = (value - high.astype(F32)).astype(BF16)
            dims = (((1,), (1,)), ((), ()))
            result = lax.dot_general(high, weight, dims, preferred_element_type=F32)
            result = result + lax.dot_general(low, weight, dims, preferred_element_type=F32)
            gx_ref[here, :] = result.astype(BF16)

        each_chunk(PIECES[p][2], 256, output)
    arrived(final.at[theirs], wc_sems.at[0], sibling)
    gw_ref[...] = final[...]
    sends.finish()


def last(back, x, weight):
    vmem, anywhere = (pl.BlockSpec(memory_space=m) for m in (pltpu.VMEM, pl.ANY))
    dma = pltpu.SemaphoreType.DMA
    n = len(PIECES)
    return pl.pallas_call(
        last_kernel,
        out_shape=(jax.ShapeDtypeStruct((ROWS, 128), BF16), jax.ShapeDtypeStruct((128, 128), F32)),
        in_specs=[anywhere, anywhere, vmem],
        out_specs=(vmem, vmem),
        scratch_shapes=[
            pltpu.VMEM((8, ROWS, 128), BF16),
            pltpu.VMEM((8, ROWS, 128), BF16),
            pltpu.VMEM((n, 2, 256, 128), BF16),
            pltpu.VMEM((n, 2, 512, 128), BF16),
            pltpu.VMEM((ROWS, 128), BF16),
            pltpu.VMEM((64, 128), F32),
            pltpu.VMEM((4, GROW, 128), F32),
            pltpu.VMEM((4, GROW, 128), F32),
            pltpu.VMEM((8, GROW, 128), F32),
            pltpu.VMEM((128, 128), F32),
            pltpu.VMEM((128, 128), F32),
            dma((2,)), dma((n, 2)), dma((n, 2)), dma((n,)), dma((48,)),
            dma((1,)), dma((4,)), dma((4,)), dma((8,)), dma((4,)), dma((1,)),
        ],
        compiler_params=pltpu.CompilerParams(
            collective_id=3, has_side_effects=True, vmem_limit_bytes=VMEM_BYTES
        ),
    )(back, x, weight)


def shards(features, weight, tile_values, tile_rows, tile_cols, tile_live, cotangent):
    tiles = tile_values[0, 0]
    rows = tile_rows[0, 0]
    cols = tile_cols[0, 0]
    live = tile_live[0]
    gathered, table = gather_row(features, tile_rows[0], tile_cols[0], live)
    layer_out, grows = middle(table, gathered.reshape(8 * ROWS, 128), weight, tiles, cotangent)
    back = backward(rows, cols, live, grows.reshape(256, 128, 128), tiles)
    grad_x, grad_w = last(back.reshape(8, ROWS, 128), gathered, weight)
    return (layer_out, grad_x, grad_w)


def solution(mesh):
    in_specs = (
        P(("col", "row"), None),
        P(),
        P("row", "col", None, None, None),
        P("row", "col", None),
        P("row", "col", None),
        P("row", "col"),
        P(("row", "col"), None),
    )
    out_specs = (P(("row", "col"), None), P(("col", "row"), None), P())
    return jax.shard_map(shards, mesh=mesh, in_specs=in_specs, out_specs=out_specs, check_vma=False)
```

```python
import functools

import jax
import jax.numpy as jnp
from jax import lax
from jax.experimental import pallas as pl
from jax.experimental.pallas import tpu as pltpu
from jax.sharding import PartitionSpec as P

MESH = pl.DeviceIdType.MESH
F32 = jnp.float32
BF16 = jnp.bfloat16
ROWS = 1024
VMEM_BYTES = 56 << 20


def place():
    r, c = lax.axis_index("row"), lax.axis_index("col")
    return (c // 2) % 4, r // 2, r % 2, c // 8, c % 2


def device(x, y, zh, zl, k):
    return (y * 2 + zh, zl * 8 + x * 2 + k)


def remote(src, dst, send, recv, target):
    return pltpu.make_async_remote_copy(
        src_ref=src, dst_ref=dst, send_sem=send, recv_sem=recv, device_id=target, device_id_type=MESH
    )


def greet(partners):
    barrier = pltpu.get_barrier_semaphore()
    for partner in partners:
        pl.semaphore_signal(barrier, inc=1, device_id=partner, device_id_type=MESH)
    pl.semaphore_wait(barrier, len(partners))


class Sends:
    def __init__(self, send_sems):
        self.sems = send_sems
        self.started = []

    def start(self, src, dst, recv, target):
        copy = remote(src, dst, self.sems.at[len(self.started)], recv, target)
        copy.start()
        self.started.append(copy)

    def finish(self):
        for copy in self.started:
            copy.wait_send()


def arrived(ref, recv, me):
    remote(ref, ref, recv, recv, me).wait_recv()


def each_chunk(rows, step, body):
    def go(i, carry):
        body(pl.ds(pl.multiple_of(i * step, step), step))
        return carry

    lax.fori_loop(0, rows // step, go, 0)


def add_into(out, terms, rows, step=128):
    def body(at):
        total = out[at, :].astype(F32)
        for term in terms:
            total = total + term[at, :].astype(F32)
        out[at, :] = total.astype(out.dtype)

    each_chunk(rows, step, body)


G1 = ((0, 0, 512), (0, 512, 512), (1, 0, 256), (1, 256, 256), (1, 512, 256), (1, 768, 256))
G1_OVER = (2, 3, 4, 5)
G1_ORDER = (("far", 0), ("near", 2), ("far", 1), ("near", 3), ("far", 2), ("near", 4), ("far", 3), ("near", 5), ("far", 4), ("far", 5))


def slot_table(rows, cols, live):
    slots = rows.shape[1]
    i = lax.broadcasted_iota(jnp.int32, (slots, slots), 0)
    lane = lax.broadcasted_iota(jnp.int32, (slots, slots), 1)
    alive = lane < live

    def upright(v):
        return jnp.sum(jnp.where(i == lane, v, 0.0), axis=1, keepdims=True)

    def number(condition, axis=1):
        return jnp.sum(jnp.where(condition, 1.0, 0.0), axis=axis, keepdims=True)

    owner = jnp.floor(rows * 0.125)
    owner_up, rows_up, cols_up = upright(owner), upright(rows), upright(cols)
    rank = number(alive & (owner == owner_up) & ((rows < rows_up) | ((rows == rows_up) & (lane < i))))
    same_row = number(alive & (rows == rows_up) & (lane < i))
    position = number(alive & ((cols < cols_up) | ((cols == cols_up) & (lane < i))))
    same_col = number(alive & (cols == cols_up) & (lane < i))
    slot = lax.broadcasted_iota(jnp.int32, (slots, 128), 0)
    entry = lax.broadcasted_iota(jnp.int32, (slots, 128), 1).astype(F32)
    chosen = jnp.where((owner_up * 4.0 + rank == entry) & (slot < live), 1.0, 0.0)
    placed = jnp.where((position == entry) & (slot < live), 1.0, 0.0)

    def pick(mask, v):
        return jnp.sum(mask * v, axis=0, keepdims=True)

    def last_of(base):
        block = entry + base
        count = number((rows_up == block) & (slot < live), 0)
        upto = number((owner_up == jnp.floor(block * 0.125)) & (rows_up <= block) & (slot < live), 0)
        return jnp.where(count > 0.0, upto - 1.0, 4.0)

    count = number((cols_up == entry) & (slot < live), 0)
    upto = number((cols_up <= entry) & (slot < live), 0)
    return (
        pick(chosen, slot.astype(F32) - 64.0) + 64.0,
        pick(chosen, rows_up - owner_up * 8.0),
        pick(chosen, cols_up),
        pick(placed, owner_up * 4.0 + rank),
        pick(placed, jnp.where(same_col > 0.0, 1.0, 0.0)),
        jnp.where(count > 0.0, upto - 1.0, 64.0),
        pick(chosen, jnp.where(same_row > 0.0, 1.0, 0.0)),
        last_of(0.0),
        last_of(128.0),
    )


def gather_row_kernel(
    live_ref, x_ref, rows_ref, cols_ref, out_ref, table_ref, local_sem, send_sems, z_sems, near_sems, far_sems
):
    x, y, zh, zl, k = place()
    right, left = device(x, (y + 1) % 4, zh, zl, k), device(x, (y + 3) % 4, zh, zl, k)
    over = device(x, y, 1 - zh, zl, k)
    greet([right, left, over])
    sends = Sends(send_sems)
    own = y * 2 + zh

    def piece(yy, p, part=None):
        side, start, size = G1[p]
        block = (yy % 4) * 2 + (1 - zh if side else zh)
        if part is not None:
            size = size // 2
            start = start + part * size
        return out_ref.at[block, pl.ds(start, size)]

    mine = pltpu.make_async_copy(x_ref, out_ref.at[own], local_sem)
    for p in G1_OVER:
        _, start, size = G1[p]
        rows = pl.ds(start, size)
        sends.start(x_ref.at[rows], out_ref.at[own, rows], z_sems.at[p], over)
    for p in (0, 1):
        _, start, size = G1[p]
        src = x_ref.at[pl.ds(start, size)]
        sends.start(src, piece(y, p), near_sems.at[p, 0], right)
        sends.start(src, piece(y, p), near_sems.at[p, 1], left)
    mine.start()

    def near(p):
        here = piece(y, p)
        arrived(here, z_sems.at[p], over)
        sends.start(here, here, near_sems.at[p, 0], right)
        sends.start(here, here, near_sems.at[p, 1], left)

    def far(p):
        arrived(piece(y + 3, p), near_sems.at[p, 0], left)
        src = piece(y + 3, p, 0)
        sends.start(src, src, far_sems.at[p, 0], right)
        arrived(piece(y + 1, p), near_sems.at[p, 1], right)
        src = piece(y + 1, p, 1)
        sends.start(src, src, far_sems.at[p, 1], left)

    table_ref[...] = jnp.zeros((16, 128), jnp.int32)
    values = slot_table(rows_ref[...].astype(F32), cols_ref[...].astype(F32), live_ref[0])
    for n, value in enumerate(values):
        table_ref[n : n + 1, :] = value.astype(jnp.int32)
    for what, p in G1_ORDER:
        (near if what == "near" else far)(p)
    for p in range(len(G1)):
        arrived(piece(y + 2, p, 0), far_sems.at[p, 0], left)
        arrived(piece(y + 2, p, 1), far_sems.at[p, 1], right)
    sends.finish()
    mine.wait()


def gather_row(features, rows, cols, live):
    n = len(G1)
    smem, vmem, anywhere = (pl.BlockSpec(memory_space=m) for m in (pltpu.SMEM, pltpu.VMEM, pl.ANY))
    return pl.pallas_call(
        gather_row_kernel,
        out_shape=(
            jax.ShapeDtypeStruct((8, ROWS, 128), BF16),
            jax.ShapeDtypeStruct((16, 128), jnp.int32),
        ),
        in_specs=[smem, anywhere, vmem, vmem],
        out_specs=(anywhere, vmem),
        scratch_shapes=[
            pltpu.SemaphoreType.DMA,
            pltpu.SemaphoreType.DMA((len(G1_OVER) + 4 * n,)),
            pltpu.SemaphoreType.DMA((n,)),
            pltpu.SemaphoreType.DMA((n, 2)),
            pltpu.SemaphoreType.DMA((n, 2)),
        ],
        compiler_params=pltpu.CompilerParams(
            collective_id=1, has_side_effects=True, vmem_limit_bytes=VMEM_BYTES
        ),
    )(live, features, rows, cols)


HALF = ROWS // 2
QUARTER = ROWS // 4
NEEDED = (
    (2, 2), (1, 2), (3, 2), (2, 1), (2, 3), (0, 2), (1, 1), (1, 3),
    (2, 0), (3, 1), (3, 3), (1, 0), (0, 1), (0, 3), (3, 0), (0, 0),
)
AHEAD = 2
PIECES = ((0, 0, 2), (0, 2, 2), (0, 4, 2), (0, 6, 2), (1, 0, 4), (1, 4, 4))
GROW = 16
ORDER = (
    ("a", 0, 2), ("a", 0, 1), ("a", 0, 3), ("b", 0, 2), ("a", 0, 0), ("b", 0, 1), ("a", 1, 2), ("b", 0, 3), ("turn", 0),
    ("c", 0, 2), ("a", 1, 1), ("b", 0, 0), ("c", 0, 1), ("turn", 1), ("a", 1, 3), ("b", 1, 2), ("c", 0, 3), ("turn", 2), ("a", 1, 0),
    ("b", 1, 1), ("c", 0, 0), ("end", 0), ("turn", 3), ("b", 1, 3), ("c", 1, 2), ("turn", 4), ("b", 1, 0), ("near", 0, 0),
    ("c", 1, 1), ("turn", 5), ("near", 0, 1), ("c", 1, 3), ("turn", 6), ("near", 0, 3), ("c", 1, 0), ("end", 1),
    ("far", 0, 0), ("near", 0, 2), ("far", 0, 1), ("near", 1, 0), ("mult", 0, 0, 0), ("turn", 7), ("mult", 0, 1, 0),
    ("far", 0, 3), ("mult", 0, 3, 0), ("near", 1, 1), ("share", 0, 0), ("mult", 0, 0, 3), ("mult", 0, 0, 1),
    ("far", 0, 2), ("near", 1, 3), ("share", 0, 1), ("mult", 0, 1, 3), ("mult", 0, 1, 1), ("mult", 0, 2, 0),
    ("far", 1, 0), ("near", 1, 2), ("share", 0, 3), ("mult", 0, 3, 3), ("mult", 0, 3, 1), ("mult", 0, 0, 2),
    ("far", 1, 1), ("share", 0, 2), ("mult", 0, 2, 3), ("mult", 0, 2, 1), ("mult", 0, 1, 2), ("mult", 0, 3, 2),
    ("mult", 0, 2, 2), ("sum", 0), ("ra", 0, 0), ("ra", 0, 1), ("ra", 0, 2), ("ra", 0, 3),
    ("far", 1, 3), ("share", 1, 0), ("wg", 0), ("mult", 1, 0, 0), ("mult", 1, 1, 0), ("rb", 0, 0), ("rb", 0, 1),
    ("far", 1, 2), ("mult", 1, 3, 0), ("mult", 1, 0, 3), ("rb", 0, 2), ("rb", 0, 3), ("ra", 0, 4), ("ra", 0, 5),
    ("share", 1, 1), ("mult", 1, 0, 1), ("mult", 1, 1, 3), ("mult", 1, 1, 1), ("rc", 0, 0), ("rc", 0, 1),
    ("mult", 1, 2, 0), ("mult", 1, 3, 3), ("mult", 1, 3, 1), ("rc", 0, 2), ("rc", 0, 3),
    ("share", 1, 3), ("mult", 1, 0, 2), ("mult", 1, 1, 2), ("rb", 0, 4), ("rb", 0, 5),
    ("mult", 1, 2, 3), ("mult", 1, 2, 1), ("mult", 1, 3, 2), ("share", 1, 2), ("mult", 1, 2, 2),
    ("sum", 1), ("ra", 1, 0), ("ra", 1, 1), ("ra", 1, 2), ("ra", 1, 3), ("wg", 1), ("wx",),
    ("rb", 1, 0), ("rb", 1, 1), ("rb", 1, 2), ("rb", 1, 3), ("rc", 1, 0), ("wy",), ("rc", 1, 1), ("ra", 1, 4),
    ("ra", 1, 5), ("rc", 1, 2), ("rc", 1, 3), ("wz",), ("rc", 0, 4), ("rc", 0, 5), ("fin", 0), ("layer",),
    ("rb", 1, 4), ("rb", 1, 5), ("ws",), ("rc", 1, 4), ("rc", 1, 5),
)


def swap(value):
    return pltpu.roll(value, 64, 1)


def lower(rows):
    return lax.broadcasted_iota(jnp.int32, (rows, 128), 1) < 64


def pack(value):
    top, bottom = value[:64], value[64:]
    low = lower(64)
    return jnp.where(low, top, swap(bottom)), jnp.where(low, swap(top), bottom)


def unpack(first, second):
    low = lower(64)
    return jnp.concatenate([jnp.where(low, first, swap(second)), jnp.where(low, swap(first), second)], axis=0)


def add_blocks(out, terms, blocks):
    def go(b, carry):
        total = out[b].astype(F32)
        for term in terms:
            total = total + term[b].astype(F32)
        out[b] = total.astype(out.dtype)
        return carry

    lax.fori_loop(0, blocks, go, 0)


def main_kernel(
    table_ref, x_ref, w_ref, tiles_ref, cot_ref, layer_ref, gx_ref, gw_ref,
    xv, proj, tiles, runs, both, sib, s1, s2, zin, cotp, layerp, grows, stage, prods, run, back, t1, t2, tz, gpp,
    xt, gacc, g8, gy4, gz8, gpart, final,
    load_sems, sib_sems, s1_sems, s2_sems, z_sems, send_sems, gz_sems, gnear_sems, gfar_sems, gsib_sems,
    t1_sems, t2_sems, tz_sems, wx_sems, wy_sems, wz_sems, wg_sems,
):
    x, y, zh, zl, k = place()
    z = zh * 4 + zl
    sibling = device(x, y, zh, zl, 1 - k)
    xs = [None] + [device((x + i) % 4, y, zh, zl, k) for i in range(1, 4)]
    ys = [None] + [device(x, (y + i) % 4, zh, zl, k) for i in range(1, 4)]
    zs = [None] + [device(x, y, ((z + i) % 8) // 4, ((z + i) % 8) % 4, k) for i in range(1, 8)]
    along = [None] + [device(x, y, zh, (zl + j) % 4, k) for j in range(1, 4)]
    over = device(x, y, 1 - zh, zl, k)
    right, left, above, below = xs[1], xs[3], ys[1], ys[3]
    first, second = pl.ds(0, QUARTER), pl.ds(QUARTER, QUARTER)

    load_x = pltpu.make_async_copy(x_ref, xv, load_sems.at[0])
    load_x.start()
    load_t = pltpu.make_async_copy(tiles_ref, tiles.at[pl.ds(0, 64)], load_sems.at[1])
    load_t.start()
    tiles[64] = jnp.zeros((128, 128), BF16)
    run[64] = jnp.zeros((64, 128), F32)
    for i in range(2):
        runs[i, 4] = jnp.zeros((2, 64, 128), BF16)
    straight = w_ref[...].astype(F32)
    twice = jnp.concatenate([straight, swap(straight)], axis=1).astype(BF16)
    load_x.wait()

    def project(i, carry):
        rows = xv[pl.ds(i * 4, 4)].reshape(512, 128)
        value = jnp.dot(rows, twice, preferred_element_type=F32).astype(BF16)
        proj[pl.ds(i * 4, 4)] = value.reshape(4, 128, 256)
        return carry

    lax.fori_loop(0, 16, project, 0)
    load_t.wait()
    greet([device((x + i % 4) % 4, y, zh, zl, (k + i // 4) % 2) for i in range(1, 8)] + ys[1:] + zs[1:])
    sends = Sends(send_sems)

    def produce(j, m):
        def side(i, carry):
            core = (1 - k) + i * (2 * k - 1)
            c = ((zl + j) % 4) * 8 + ((x + m) % 4) * 2 + core
            low = lower(64)
            before = None
            for n in range(4):
                entry = c * 4 + n
                value = jnp.dot(tiles[table_ref[0, entry]], proj[table_ref[2, entry]], preferred_element_type=F32)
                value = (
                    jnp.where(low, value[:64, :128], value[64:, 128:]),
                    jnp.where(low, value[:64, 128:], value[64:, :128]),
                )
                if n:
                    same = table_ref[6, entry] == 1
                    value = tuple(v + jnp.where(same, u, 0.0) for v, u in zip(value, before))
                for q in range(2):
                    runs[i, n, q] = value[q].astype(BF16)
                before = value
            for b in range(8):
                at = table_ref[7 + c // 16, (c % 16) * 8 + b]
                for q in range(2):
                    both[i, q, j, m, pl.ds(b * 64, 64), :] = runs[i, at, q]
            return carry

        lax.fori_loop(0, 2, side, 0)
        for q in range(2):
            sends.start(both.at[0, q, j, m], sib.at[q, j, m], sib_sems.at[j, m, q], sibling)

    produced = []

    def joined(j, m, q):
        while len(produced) < len(NEEDED) and len(produced) <= NEEDED.index((j, m)) + AHEAD:
            produce(*NEEDED[len(produced)])
            produced.append(True)
        arrived(sib.at[q, j, m], sib_sems.at[j, m, q], sibling)

    def step_a(q, j):
        joined(j, 2, q)
        add_into(both.at[1, q, j, 2], [sib.at[q, j, 2]], HALF)
        sends.start(both.at[1, q, j, 2, first], s1.at[q, j, 0], s1_sems.at[q, j, 0], right)
        sends.start(both.at[1, q, j, 2, second], s1.at[q, j, 1], s1_sems.at[q, j, 1], left)

    def step_b(q, j):
        for m, side, near, far, target, source in ((1, 0, first, second, right, left), (3, 1, second, first, left, right)):
            joined(j, m, q)
            mine = both.at[1, q, j, m]
            add_into(mine.at[far], [sib.at[q, j, m, far]], QUARTER)
            arrived(s1.at[q, j, side], s1_sems.at[q, j, side], source)
            add_into(mine.at[near], [sib.at[q, j, m, near], s1.at[q, j, side]], QUARTER)
            sends.start(mine, s2.at[q, j, side], s2_sems.at[q, j, side], target)

    def step_c(q, j):
        joined(j, 0, q)
        arrived(s2.at[q, j, 0], s2_sems.at[q, j, 0], left)
        arrived(s2.at[q, j, 1], s2_sems.at[q, j, 1], right)
        if j:
            mine = both.at[1, q, j, 0]
            add_into(mine, [sib.at[q, j, 0], s2.at[q, j, 0], s2.at[q, j, 1]], HALF)
            sends.start(mine, zin.at[q, j - 1], z_sems.at[q, j - 1], along[j])

    def place_of(j, m, core):
        return ((zl + 4 - j) % 4) * 8 + ((x + m) % 4) * 2 + core

    def block(q, j, m, part=None, core=None):
        at = grows.at[q, place_of(j, m, k if core is None else core)]
        return at if part is None else at.at[pl.ds(part * 4, 4)]

    def pack_cotangent():
        def go(b, carry):
            value = cot_ref[pl.ds(pl.multiple_of(b * 128, 128), 128), :].astype(F32)
            for q, part in enumerate(pack(value)):
                cotp[q, pl.ds(pl.multiple_of(b * 64, 64), 64), :] = part
            return carry

        lax.fori_loop(0, 8, go, 0)

    def end(q):
        if q == 0:
            pack_cotangent()
        for j in range(1, 4):
            arrived(zin.at[q, j - 1], z_sems.at[q, j - 1], along[4 - j])
        here = place_of(0, 0, k)

        def finish(b, carry):
            at = pl.ds(pl.multiple_of(b * 64, 64), 64)
            pre = both[1, q, 0, 0, at, :].astype(F32) + sib[q, 0, 0, at, :].astype(F32)
            for term in (s2.at[q, 0, 0], s2.at[q, 0, 1], zin.at[q, 0], zin.at[q, 1], zin.at[q, 2]):
                pre = pre + term[at, :].astype(F32)
            sigma = jax.nn.sigmoid(pre)
            layerp[q, at, :] = pre * sigma
            slope = sigma * (1.0 + pre * (1.0 - sigma))
            grows[q, here, b] = (cotp[q, at, :] * slope).astype(BF16)
            return carry

        lax.fori_loop(0, 8, finish, 0)
        for j in (1, 3, 2):
            sends.start(block(q, 0, 0), block(q, 0, 0), gz_sems.at[q, j - 1], along[j])

    def layer():
        def go(b, carry):
            at = pl.ds(pl.multiple_of(b * 64, 64), 64)
            value = unpack(layerp[0, at, :], layerp[1, at, :])
            layer_ref[pl.ds(pl.multiple_of(b * 128, 128), 128), :] = value.astype(BF16)
            return carry

        lax.fori_loop(0, 8, go, 0)

    def near(q, j):
        src = block(q, j, 0)
        if j:
            arrived(src, gz_sems.at[q, j - 1], along[4 - j])
        sends.start(src, src, gnear_sems.at[q, j, 0], right)
        sends.start(src, src, gnear_sems.at[q, j, 1], left)
        sends.start(src, src, gsib_sems.at[q, j, 0], sibling)

    def far(q, j):
        arrived(block(q, j, 3), gnear_sems.at[q, j, 0], left)
        sends.start(block(q, j, 3, 0), block(q, j, 3, 0), gfar_sems.at[q, j, 0], right)
        arrived(block(q, j, 1), gnear_sems.at[q, j, 1], right)
        sends.start(block(q, j, 1, 1), block(q, j, 1, 1), gfar_sems.at[q, j, 1], left)
        sends.start(block(q, j, 3), block(q, j, 3), gsib_sems.at[q, j, 1], sibling)
        sends.start(block(q, j, 1), block(q, j, 1), gsib_sems.at[q, j, 2], sibling)

    def share(q, j):
        arrived(block(q, j, 2, 0), gfar_sems.at[q, j, 0], left)
        sends.start(block(q, j, 2, 0), block(q, j, 2, 0), gsib_sems.at[q, j, 3], sibling)
        arrived(block(q, j, 2, 1), gfar_sems.at[q, j, 1], right)
        sends.start(block(q, j, 2, 1), block(q, j, 2, 1), gsib_sems.at[q, j, 4], sibling)

    def mult(q, j, m):
        if m == 2:
            arrived(block(q, j, 2, 0, 1 - k), gsib_sems.at[q, j, 3], sibling)
            arrived(block(q, j, 2, 1, 1 - k), gsib_sems.at[q, j, 4], sibling)
        else:
            arrived(block(q, j, m, None, 1 - k), gsib_sems.at[q, j, {0: 0, 3: 1, 1: 2}[m]], sibling)

        def go(i, carry):
            c = place_of(j, m, i)
            stage[...] = grows[q, c]
            for n in range(4):
                entry = c * 4 + n
                part = stage[table_ref[1, entry]].astype(F32)
                other = swap(part)
                part = jnp.concatenate(
                    [jnp.concatenate([part, other], axis=1), jnp.concatenate([other, part], axis=1)], axis=0
                ).astype(BF16)
                value = lax.dot_general(
                    tiles[table_ref[0, entry]], part, (((0,), (0,)), ((), ())), preferred_element_type=F32
                )
                prods[q, entry] = jnp.where(lower(64), value[:64, :128], value[64:, 128:])
            return carry

        lax.fori_loop(0, 2, go, 0)

    def add_up(q):
        run[0] = prods[q, table_ref[3, 0]]

        def go(p, carry):
            run[p] = prods[q, table_ref[3, p]] + jnp.where(table_ref[4, p] == 1, run[p - 1], 0.0)
            return carry

        lax.fori_loop(1, 64, go, 0)

        def place_block(r, carry):
            for b in range(8):
                back[q, r, b] = run[table_ref[5, r * 8 + b]].astype(BF16)
            return carry

        lax.fori_loop(0, 8, place_block, 0)

    def dest(m, p):
        return ((y + m) % 4) * 2 + (zh if PIECES[p][0] else 1 - zh)

    def mine_of(q, m, p, part=None):
        _, start, size = PIECES[p]
        if part is not None:
            size = size // 2
            start = start + part * size
        return back.at[q, dest(m, p), pl.ds(start, size)]

    def t1_of(q, p, side):
        return t1.at[q, p, side, pl.ds(0, PIECES[p][2] // 2)]

    def t2_of(q, p, side):
        return t2.at[q, p, side, pl.ds(0, PIECES[p][2])]

    def row_a(q, p):
        sends.start(mine_of(q, 2, p, 0), t1_of(q, p, 0), t1_sems.at[q, p, 0], above)
        sends.start(mine_of(q, 2, p, 1), t1_of(q, p, 1), t1_sems.at[q, p, 1], below)

    def row_b(q, p):
        for m, side, target, source in ((1, 0, above, below), (3, 1, below, above)):
            arrived(t1_of(q, p, side), t1_sems.at[q, p, side], source)
            add_blocks(mine_of(q, m, p, side), [t1_of(q, p, side)], PIECES[p][2] // 2)
            sends.start(mine_of(q, m, p), t2_of(q, p, side), t2_sems.at[q, p, side], target)

    def row_c(q, p):
        arrived(t2_of(q, p, 0), t2_sems.at[q, p, 0], below)
        arrived(t2_of(q, p, 1), t2_sems.at[q, p, 1], above)
        if PIECES[p][0] == 0:
            add_blocks(mine_of(q, 0, p), [t2_of(q, p, 0), t2_of(q, p, 1)], PIECES[p][2])
            _, start, size = PIECES[p]
            sends.start(mine_of(q, 0, p), tz.at[q, pl.ds(start, size)], tz_sems.at[q, p], over)

    def row_end(q):
        for p in range(4):
            _, start, size = PIECES[p]
            arrived(tz.at[q, pl.ds(start, size)], tz_sems.at[q, p], over)
        for p in (4, 5):
            _, start, size = PIECES[p]

            def go(b, carry):
                value = back[q, dest(0, p), start + b].astype(F32) + tz[q, start + b].astype(F32)
                gpp[q, start + b] = value + t2[q, p, 0, b].astype(F32) + t2[q, p, 1, b].astype(F32)
                return carry

            lax.fori_loop(0, size, go, 0)

    eight = [None] + [device((x + i) % 4, y, zh, zl, (k + i // 4) % 2) for i in range(1, 8)]

    def back_of(i):
        return i // 4 * 4 + (4 - i % 4) % 4

    def part_of(i):
        return pl.ds(((k + i // 4) % 2) * 64 + ((x + i) % 4) * GROW, GROW)

    slice_ = part_of(0)

    def turn(part):
        def go(i, carry):
            b = part * 4 + i
            one = xv[b * 2].astype(F32).T
            two = xv[b * 2 + 1].astype(F32).T
            low = lower(128)
            xt[b, :128] = jnp.where(low, one, swap(two)).astype(BF16)
            xt[b, 128:] = jnp.where(low, swap(one), two).astype(BF16)
            return carry

        lax.fori_loop(0, 4, go, 0)

    def weight_grad(q):
        total = jnp.zeros((256, 128), F32)
        for b in range(32):
            nodes = back[q, b // 4, pl.ds((b % 4) * 2, 2)].reshape(128, 128)
            total = total + jnp.dot(xt[b], nodes, preferred_element_type=F32)
        gacc[q] = jnp.where(lower(128), total[:128] + swap(total[128:]), 0.0)

    def weight_x():
        gpart[...] = gacc[0] + swap(gacc[1])
        for i in range(8):
            if i:
                sends.start(gpart.at[part_of(i)], g8.at[i], wx_sems.at[i], eight[i])

    def weight_y():
        total = gpart[slice_, :]
        for i in range(1, 8):
            arrived(g8.at[i], wx_sems.at[i], eight[back_of(i)])
            total = total + g8[i]
        g8[0] = total
        for i in range(1, 4):
            sends.start(g8.at[0], gy4.at[i], wy_sems.at[i], ys[i])

    def weight_z():
        for i in range(1, 4):
            arrived(gy4.at[i], wy_sems.at[i], ys[4 - i])
        gy4[0] = g8[0] + gy4[1] + gy4[2] + gy4[3]
        for i in range(1, 8):
            sends.start(gy4.at[0], gz8.at[i], wz_sems.at[i], zs[i])

    def weight_share():
        for i in range(1, 8):
            arrived(gz8.at[i], wz_sems.at[i], zs[8 - i])
        total = gy4[0]
        for i in range(1, 8):
            total = total + gz8[i]
        final[slice_, :] = total
        for i in range(1, 8):
            sends.start(final.at[slice_], final.at[slice_], wg_sems.at[i], eight[i])

    steps = {
        "a": step_a, "b": step_b, "c": step_c, "end": end, "near": near, "far": far, "share": share, "mult": mult,
        "sum": add_up, "ra": row_a, "rb": row_b, "rc": row_c, "fin": row_end, "layer": layer,
        "turn": turn, "wg": weight_grad, "wx": weight_x, "wy": weight_y, "wz": weight_z, "ws": weight_share,
    }
    for name, *which in ORDER:
        steps[name](*which)
    row_end(1)
    weight = w_ref[...]

    def output(b, carry):
        value = unpack(gpp[0, b], gpp[1, b])
        high = value.astype(BF16)
        low = (value - high.astype(F32)).astype(BF16)
        dims = (((1,), (1,)), ((), ()))
        result = lax.dot_general(high, weight, dims, preferred_element_type=F32)
        result = result + lax.dot_general(low, weight, dims, preferred_element_type=F32)
        gx_ref[pl.ds(pl.multiple_of(b * 128, 128), 128), :] = result.astype(BF16)
        return carry

    lax.fori_loop(0, 8, output, 0)
    for i in range(1, 8):
        arrived(final.at[part_of(back_of(i))], wg_sems.at[i], eight[back_of(i)])
    gw_ref[...] = final[...]
    sends.finish()


def main(table, x, weight, tiles, cotangent):
    smem, vmem, anywhere = (pl.BlockSpec(memory_space=m) for m in (pltpu.SMEM, pltpu.VMEM, pl.ANY))
    dma = pltpu.SemaphoreType.DMA
    n = len(PIECES)
    return pl.pallas_call(
        main_kernel,
        out_shape=(
            jax.ShapeDtypeStruct((ROWS, 128), BF16),
            jax.ShapeDtypeStruct((ROWS, 128), BF16),
            jax.ShapeDtypeStruct((128, 128), F32),
        ),
        in_specs=[smem, anywhere, vmem, anywhere, vmem],
        out_specs=(vmem, vmem, vmem),
        scratch_shapes=[
            pltpu.VMEM((64, 128, 128), BF16),
            pltpu.VMEM((64, 128, 256), BF16),
            pltpu.VMEM((65, 128, 128), BF16),
            pltpu.VMEM((2, 5, 2, 64, 128), BF16),
            pltpu.VMEM((2, 2, 4, 4, HALF, 128), BF16),
            pltpu.VMEM((2, 4, 4, HALF, 128), BF16),
            pltpu.VMEM((2, 4, 2, QUARTER, 128), BF16),
            pltpu.VMEM((2, 4, 2, HALF, 128), BF16),
            pltpu.VMEM((2, 3, HALF, 128), BF16),
            pltpu.VMEM((2, HALF, 128), F32),
            pltpu.VMEM((2, HALF, 128), F32),
            pltpu.VMEM((2, 32, 8, 64, 128), BF16),
            pltpu.VMEM((8, 64, 128), BF16),
            pltpu.VMEM((2, 128, 64, 128), F32),
            pltpu.VMEM((65, 64, 128), F32),
            pltpu.VMEM((2, 8, 8, 64, 128), BF16),
            pltpu.VMEM((2, n, 2, 2, 64, 128), BF16),
            pltpu.VMEM((2, n, 2, 4, 64, 128), BF16),
            pltpu.VMEM((2, 8, 64, 128), BF16),
            pltpu.VMEM((2, 8, 64, 128), F32),
            pltpu.VMEM((32, 256, 128), BF16),
            pltpu.VMEM((2, 128, 128), F32),
            pltpu.VMEM((8, GROW, 128), F32),
            pltpu.VMEM((4, GROW, 128), F32),
            pltpu.VMEM((8, GROW, 128), F32),
            pltpu.VMEM((128, 128), F32),
            pltpu.VMEM((128, 128), F32),
            dma((2,)), dma((4, 4, 2)), dma((2, 4, 2)), dma((2, 4, 2)), dma((2, 3)), dma((256,)),
            dma((2, 3)), dma((2, 4, 2)), dma((2, 4, 2)), dma((2, 4, 5)),
            dma((2, n, 2)), dma((2, n, 2)), dma((2, n)),
            dma((8,)), dma((4,)), dma((8,)), dma((8,)),
        ],
        compiler_params=pltpu.CompilerParams(
            collective_id=2, has_side_effects=True, vmem_limit_bytes=VMEM_BYTES
        ),
    )(table, x, weight, tiles, cotangent)


def shards(features, weight, tile_values, tile_rows, tile_cols, tile_live, cotangent):
    gathered, table = gather_row(features, tile_rows[0], tile_cols[0], tile_live[0])
    return main(table, gathered.reshape(64, 128, 128), weight, tile_values[0, 0], cotangent)


def solution(mesh):
    in_specs = (
        P(("col", "row"), None),
        P(),
        P("row", "col", None, None, None),
        P("row", "col", None),
        P("row", "col", None),
        P("row", "col"),
        P(("row", "col"), None),
    )
    out_specs = (P(("row", "col"), None), P(("col", "row"), None), P())
    return jax.shard_map(shards, mesh=mesh, in_specs=in_specs, out_specs=out_specs, check_vma=False)
```

```python
import functools

import jax
import jax.numpy as jnp
from jax import lax
from jax.experimental import pallas as pl
from jax.experimental.pallas import tpu as pltpu
from jax.sharding import PartitionSpec as P

MESH = pl.DeviceIdType.MESH
F32 = jnp.float32
BF16 = jnp.bfloat16
ROWS = 1024
VMEM_BYTES = 56 << 20


def place():
    r, c = lax.axis_index("row"), lax.axis_index("col")
    return (c // 2) % 4, r // 2, r % 2, c // 8, c % 2


def device(x, y, zh, zl, k):
    return (y * 2 + zh, zl * 8 + x * 2 + k)


def remote(src, dst, send, recv, target):
    return pltpu.make_async_remote_copy(
        src_ref=src, dst_ref=dst, send_sem=send, recv_sem=recv, device_id=target, device_id_type=MESH
    )


def greet(partners):
    barrier = pltpu.get_barrier_semaphore()
    for partner in partners:
        pl.semaphore_signal(barrier, inc=1, device_id=partner, device_id_type=MESH)


def greeted(partners):
    pl.semaphore_wait(pltpu.get_barrier_semaphore(), len(partners))


class Sends:
    def __init__(self, send_sems):
        self.sems = send_sems
        self.started = []

    def start(self, src, dst, recv, target):
        copy = remote(src, dst, self.sems.at[len(self.started)], recv, target)
        copy.start()
        self.started.append(copy)

    def finish(self):
        for copy in self.started:
            copy.wait_send()


def arrived(ref, recv, me):
    remote(ref, ref, recv, recv, me).wait_recv()


def each_chunk(rows, step, body):
    def go(i, carry):
        body(pl.ds(pl.multiple_of(i * step, step), step))
        return carry

    lax.fori_loop(0, rows // step, go, 0)


def add_into(out, terms, rows, step=128):
    def body(at):
        total = out[at, :].astype(F32)
        for term in terms:
            total = total + term[at, :].astype(F32)
        out[at, :] = total.astype(out.dtype)

    each_chunk(rows, step, body)


def slot_table(rows, cols, live):
    slots = rows.shape[1]
    i = lax.broadcasted_iota(jnp.int32, (slots, slots), 0)
    lane = lax.broadcasted_iota(jnp.int32, (slots, slots), 1)
    alive = lane < live

    def upright(v):
        return jnp.sum(jnp.where(i == lane, v, 0.0), axis=1, keepdims=True)

    def number(condition, axis=1):
        return jnp.sum(jnp.where(condition, 1.0, 0.0), axis=axis, keepdims=True)

    owner = jnp.floor(rows * 0.125)
    owner_up, rows_up, cols_up = upright(owner), upright(rows), upright(cols)
    rank = number(alive & (owner == owner_up) & ((rows < rows_up) | ((rows == rows_up) & (lane < i))))
    same_row = number(alive & (rows == rows_up) & (lane < i))
    position = number(alive & ((cols < cols_up) | ((cols == cols_up) & (lane < i))))
    same_col = number(alive & (cols == cols_up) & (lane < i))
    slot = lax.broadcasted_iota(jnp.int32, (slots, 128), 0)
    entry = lax.broadcasted_iota(jnp.int32, (slots, 128), 1).astype(F32)
    chosen = jnp.where((owner_up * 4.0 + rank == entry) & (slot < live), 1.0, 0.0)
    placed = jnp.where((position == entry) & (slot < live), 1.0, 0.0)

    def pick(mask, v):
        return jnp.sum(mask * v, axis=0, keepdims=True)

    owners = jnp.where((owner_up == entry) & (slot < live), 1.0, 0.0).astype(BF16)
    offset = rows_up - owner_up * 8.0

    def per_owner(condition):
        ones = jnp.where(condition, 1.0, 0.0).astype(BF16)
        return lax.dot_general(owners, ones, (((0,), (0,)), ((), ())), preferred_element_type=F32)[:32]

    block_count, block_upto = per_owner(offset == entry), per_owner(offset <= entry)
    count = number((cols_up == entry) & (slot < live), 0)
    upto = number((cols_up <= entry) & (slot < live), 0)
    return (
        pick(chosen, slot.astype(F32) - 64.0) + 64.0,
        pick(chosen, rows_up - owner_up * 8.0),
        pick(chosen, cols_up),
        pick(placed, owner_up * 4.0 + rank),
        pick(placed, jnp.where(same_col > 0.0, 1.0, 0.0)),
        jnp.where(count > 0.0, upto - 1.0, 64.0),
        pick(chosen, jnp.where(same_row > 0.0, 1.0, 0.0)),
    ), jnp.where(block_count > 0.0, block_upto - 1.0, 4.0)


def table_kernel(live_ref, rows_ref, cols_ref, table_ref):
    table_ref[...] = jnp.zeros((40, 128), jnp.int32)
    lists, blocks = slot_table(rows_ref[...].astype(F32), cols_ref[...].astype(F32), live_ref[0])
    for n, value in enumerate(lists):
        table_ref[n : n + 1, :] = value.astype(jnp.int32)
    table_ref[8:40, :] = blocks.astype(jnp.int32)


def make_table(live, rows, cols):
    smem, vmem = (pl.BlockSpec(memory_space=m) for m in (pltpu.SMEM, pltpu.VMEM))
    return pl.pallas_call(
        table_kernel,
        out_shape=jax.ShapeDtypeStruct((40, 128), jnp.int32),
        in_specs=[smem, vmem, vmem],
        out_specs=vmem,
    )(live, rows, cols)


HALF = ROWS // 2
QUARTER = ROWS // 4
NEEDED = (
    (2, 2), (1, 2), (3, 2), (2, 1), (2, 3), (0, 2), (1, 1), (1, 3),
    (2, 0), (3, 1), (3, 3), (1, 0), (0, 1), (0, 3), (3, 0), (0, 0),
)
AHEAD = 1
PIECES = ((0, 0, 2), (0, 2, 2), (0, 4, 2), (0, 6, 2), (1, 0, 4), (1, 4, 4))
GROW = 16
GATHER = ((0, 0, 4), (0, 4, 4), (1, 0, 2), (1, 2, 2), (1, 4, 2), (1, 6, 2))
ORDER = (
    ("gz", 2), ("gz", 3), ("gz", 4), ("gz", 5), ("gown",), ("gfar", 0), ("gnear", 2), ("gfar", 1), ("gnear", 3), ("gfar", 2),
    ("gnear", 4), ("gfar", 3), ("gnear", 5), ("gfar", 4), ("gfar", 5), ("gdone",),
    ("a", 0, 2), ("a", 0, 1), ("a", 0, 3), ("b", 0, 2), ("a", 0, 0), ("b", 0, 1), ("a", 1, 2), ("b", 0, 3), ("turn", 0),
    ("c", 0, 2), ("a", 1, 1), ("b", 0, 0), ("c", 0, 1), ("turn", 1), ("a", 1, 3), ("b", 1, 2), ("c", 0, 3), ("turn", 2), ("a", 1, 0),
    ("b", 1, 1), ("c", 0, 0), ("end", 0), ("turn", 3), ("b", 1, 3), ("c", 1, 2), ("turn", 4), ("b", 1, 0), ("near", 0, 0),
    ("c", 1, 1), ("turn", 5), ("near", 0, 1), ("c", 1, 3), ("turn", 6), ("near", 0, 3), ("c", 1, 0), ("end", 1),
    ("far", 0, 0), ("near", 0, 2), ("far", 0, 1), ("near", 1, 0), ("mult", 0, 0, 0), ("turn", 7), ("mult", 0, 1, 0),
    ("far", 0, 3), ("mult", 0, 3, 0), ("near", 1, 1), ("share", 0, 0), ("mult", 0, 0, 3), ("mult", 0, 0, 1),
    ("far", 0, 2), ("near", 1, 3), ("share", 0, 1), ("mult", 0, 1, 3), ("mult", 0, 1, 1), ("mult", 0, 2, 0),
    ("far", 1, 0), ("near", 1, 2), ("share", 0, 3), ("mult", 0, 3, 3), ("mult", 0, 3, 1), ("mult", 0, 0, 2),
    ("far", 1, 1), ("share", 0, 2), ("mult", 0, 2, 3), ("mult", 0, 2, 1), ("mult", 0, 1, 2), ("mult", 0, 3, 2),
    ("mult", 0, 2, 2), ("sum", 0), ("ra", 0, 0), ("ra", 0, 1), ("ra", 0, 2), ("ra", 0, 3),
    ("far", 1, 3), ("share", 1, 0), ("wg", 0), ("mult", 1, 0, 0), ("mult", 1, 1, 0), ("rb", 0, 0), ("rb", 0, 1),
    ("far", 1, 2), ("mult", 1, 3, 0), ("mult", 1, 0, 3), ("rb", 0, 2), ("rb", 0, 3), ("ra", 0, 4), ("ra", 0, 5),
    ("share", 1, 1), ("mult", 1, 0, 1), ("mult", 1, 1, 3), ("mult", 1, 1, 1), ("rc", 0, 0), ("rc", 0, 1),
    ("mult", 1, 2, 0), ("mult", 1, 3, 3), ("mult", 1, 3, 1), ("rc", 0, 2), ("rc", 0, 3),
    ("share", 1, 3), ("mult", 1, 0, 2), ("mult", 1, 1, 2), ("rb", 0, 4), ("rb", 0, 5),
    ("mult", 1, 2, 3), ("mult", 1, 2, 1), ("mult", 1, 3, 2), ("share", 1, 2), ("mult", 1, 2, 2),
    ("sum", 1), ("ra", 1, 0), ("ra", 1, 1), ("ra", 1, 2), ("ra", 1, 3), ("wg", 1), ("wx",),
    ("rb", 1, 0), ("rb", 1, 1), ("rb", 1, 2), ("rb", 1, 3), ("rc", 1, 0), ("wy",), ("rc", 1, 1), ("ra", 1, 4),
    ("ra", 1, 5), ("rc", 1, 2), ("rc", 1, 3), ("wz",), ("rc", 0, 4), ("rc", 0, 5), ("fin", 0), ("layer",),
    ("rb", 1, 4), ("rb", 1, 5), ("ws",), ("rc", 1, 4), ("rc", 1, 5),
)


def swap(value):
    return pltpu.roll(value, 64, 1)


def lower(rows):
    return lax.broadcasted_iota(jnp.int32, (rows, 128), 1) < 64


def pack(value):
    top, bottom = value[:64], value[64:]
    low = lower(64)
    return jnp.where(low, top, swap(bottom)), jnp.where(low, swap(top), bottom)


def unpack(first, second):
    low = lower(64)
    return jnp.concatenate([jnp.where(low, first, swap(second)), jnp.where(low, swap(first), second)], axis=0)


def add_blocks(out, terms, blocks):
    def go(b, carry):
        total = out[b].astype(F32)
        for term in terms:
            total = total + term[b].astype(F32)
        out[b] = total.astype(out.dtype)
        return carry

    lax.fori_loop(0, blocks, go, 0)


def main_kernel(
    table_ref, x_ref, w_ref, tiles_ref, cot_ref, layer_ref, gx_ref, gw_ref,
    xv, proj, tiles, runs, both, sib, s1, s2, zin, cotp, layerp, grows, stage, prods, run, back, t1, t2, tz, gpp,
    xt, gacc, g8, gy4, gz8, gpart, final,
    load_sems, gz_row, gnear_row, gfar_row, sib_sems, s1_sems, s2_sems, z_sems, send_sems, gz_sems, gnear_sems, gfar_sems, gsib_sems,
    t1_sems, t2_sems, tz_sems, wx_sems, wy_sems, wz_sems, wg_sems,
):
    x, y, zh, zl, k = place()
    z = zh * 4 + zl
    sibling = device(x, y, zh, zl, 1 - k)
    xs = [None] + [device((x + i) % 4, y, zh, zl, k) for i in range(1, 4)]
    ys = [None] + [device(x, (y + i) % 4, zh, zl, k) for i in range(1, 4)]
    zs = [None] + [device(x, y, ((z + i) % 8) // 4, ((z + i) % 8) % 4, k) for i in range(1, 8)]
    along = [None] + [device(x, y, zh, (zl + j) % 4, k) for j in range(1, 4)]
    over = device(x, y, 1 - zh, zl, k)
    right, left, above, below = xs[1], xs[3], ys[1], ys[3]
    first, second = pl.ds(0, QUARTER), pl.ds(QUARTER, QUARTER)

    partners = [device((x + i % 4) % 4, y, zh, zl, (k + i // 4) % 2) for i in range(1, 8)] + ys[1:] + zs[1:]
    here_row = y * 2 + zh
    load_x = pltpu.make_async_copy(x_ref, xv.at[here_row], load_sems.at[0])
    load_x.start()
    load_t = pltpu.make_async_copy(tiles_ref, tiles.at[pl.ds(0, 64)], load_sems.at[1])
    load_t.start()
    greet(partners)

    straight = w_ref[...].astype(F32)
    twice = jnp.concatenate([straight, swap(straight)], axis=1).astype(BF16)
    greeted(partners)
    sends = Sends(send_sems)

    def gather_at(yy, p, part=None):
        side, start, size = GATHER[p]
        row = (yy % 4) * 2 + (1 - zh if side else zh)
        if part is not None:
            size = size // 2
            start = start + part * size
        return row, start, size

    def gathered(yy, p, part=None):
        row, start, size = gather_at(yy, p, part)
        return xv.at[row, pl.ds(start, size)]

    def project(yy, p, part=None):
        row, start, size = gather_at(yy, p, part)
        nodes = xv[row, pl.ds(start, size)].reshape(size * 128, 128)
        value = jnp.dot(nodes, twice, preferred_element_type=F32).astype(BF16)
        proj[pl.ds(row * 8 + start, size)] = value.reshape(size, 128, 256)

    def gather_z(p):
        _, start, size = GATHER[p]
        src = x_ref.at[pl.ds(start, size)]
        sends.start(src, xv.at[here_row, pl.ds(start, size)], gz_row.at[p], over)

    def gather_own():
        for p in (0, 1):
            _, start, size = GATHER[p]
            src = x_ref.at[pl.ds(start, size)]
            sends.start(src, gathered(y, p), gnear_row.at[p, 0], above)
            sends.start(src, gathered(y, p), gnear_row.at[p, 1], below)
        tiles[64] = jnp.zeros((128, 128), BF16)
        run[64] = jnp.zeros((64, 128), F32)
        for i in range(2):
            runs[i, 4] = jnp.zeros((2, 64, 128), BF16)
        load_x.wait()
        for p in (0, 1):
            project(y, p)
        load_t.wait()

    def gather_near(p):
        arrived(gathered(y, p), gz_row.at[p], over)
        sends.start(gathered(y, p), gathered(y, p), gnear_row.at[p, 0], above)
        sends.start(gathered(y, p), gathered(y, p), gnear_row.at[p, 1], below)
        project(y, p)

    def gather_far(p):
        arrived(gathered(y + 3, p), gnear_row.at[p, 0], below)
        sends.start(gathered(y + 3, p, 0), gathered(y + 3, p, 0), gfar_row.at[p, 0], above)
        arrived(gathered(y + 1, p), gnear_row.at[p, 1], above)
        sends.start(gathered(y + 1, p, 1), gathered(y + 1, p, 1), gfar_row.at[p, 1], below)
        project(y + 3, p)
        project(y + 1, p)

    def gather_done():
        for p in range(len(GATHER)):
            arrived(gathered(y + 2, p, 0), gfar_row.at[p, 0], below)
            arrived(gathered(y + 2, p, 1), gfar_row.at[p, 1], above)
            project(y + 2, p)

    def produce(j, m):
        def side(i, carry):
            core = (1 - k) + i * (2 * k - 1)
            c = ((zl + j) % 4) * 8 + ((x + m) % 4) * 2 + core
            low = lower(64)
            before = None
            for n in range(4):
                entry = c * 4 + n
                value = jnp.dot(tiles[table_ref[0, entry]], proj[table_ref[2, entry]], preferred_element_type=F32)
                value = (
                    jnp.where(low, value[:64, :128], value[64:, 128:]),
                    jnp.where(low, value[:64, 128:], value[64:, :128]),
                )
                if n:
                    same = table_ref[6, entry] == 1
                    value = tuple(v + jnp.where(same, u, 0.0) for v, u in zip(value, before))
                for q in range(2):
                    runs[i, n, q] = value[q].astype(BF16)
                before = value
            for b in range(8):
                at = table_ref[8 + c, b]
                for q in range(2):
                    both[i, q, j, m, pl.ds(b * 64, 64), :] = runs[i, at, q]
            return carry

        lax.fori_loop(0, 2, side, 0)
        for q in range(2):
            sends.start(both.at[0, q, j, m], sib.at[q, j, m], sib_sems.at[j, m, q], sibling)

    produced = []

    def joined(j, m, q):
        while len(produced) < len(NEEDED) and len(produced) <= NEEDED.index((j, m)) + AHEAD:
            produce(*NEEDED[len(produced)])
            produced.append(True)
        arrived(sib.at[q, j, m], sib_sems.at[j, m, q], sibling)

    def step_a(q, j):
        joined(j, 2, q)
        add_into(both.at[1, q, j, 2], [sib.at[q, j, 2]], HALF)
        sends.start(both.at[1, q, j, 2, first], s1.at[q, j, 0], s1_sems.at[q, j, 0], right)
        sends.start(both.at[1, q, j, 2, second], s1.at[q, j, 1], s1_sems.at[q, j, 1], left)

    def step_b(q, j):
        for m, side, near, far, target, source in ((1, 0, first, second, right, left), (3, 1, second, first, left, right)):
            joined(j, m, q)
            mine = both.at[1, q, j, m]
            add_into(mine.at[far], [sib.at[q, j, m, far]], QUARTER)
            arrived(s1.at[q, j, side], s1_sems.at[q, j, side], source)
            add_into(mine.at[near], [sib.at[q, j, m, near], s1.at[q, j, side]], QUARTER)
            sends.start(mine, s2.at[q, j, side], s2_sems.at[q, j, side], target)

    def step_c(q, j):
        joined(j, 0, q)
        arrived(s2.at[q, j, 0], s2_sems.at[q, j, 0], left)
        arrived(s2.at[q, j, 1], s2_sems.at[q, j, 1], right)
        if j:
            mine = both.at[1, q, j, 0]
            add_into(mine, [sib.at[q, j, 0], s2.at[q, j, 0], s2.at[q, j, 1]], HALF)
            sends.start(mine, zin.at[q, j - 1], z_sems.at[q, j - 1], along[j])

    def place_of(j, m, core):
        return ((zl + 4 - j) % 4) * 8 + ((x + m) % 4) * 2 + core

    def block(q, j, m, part=None, core=None):
        at = grows.at[q, place_of(j, m, k if core is None else core)]
        return at if part is None else at.at[pl.ds(part * 4, 4)]

    def pack_cotangent():
        def go(b, carry):
            value = cot_ref[pl.ds(pl.multiple_of(b * 128, 128), 128), :].astype(F32)
            for q, part in enumerate(pack(value)):
                cotp[q, pl.ds(pl.multiple_of(b * 64, 64), 64), :] = part
            return carry

        lax.fori_loop(0, 8, go, 0)

    def end(q):
        if q == 0:
            pack_cotangent()
        for j in range(1, 4):
            arrived(zin.at[q, j - 1], z_sems.at[q, j - 1], along[4 - j])
        here = place_of(0, 0, k)

        def finish(b, carry):
            at = pl.ds(pl.multiple_of(b * 64, 64), 64)
            pre = both[1, q, 0, 0, at, :].astype(F32) + sib[q, 0, 0, at, :].astype(F32)
            for term in (s2.at[q, 0, 0], s2.at[q, 0, 1], zin.at[q, 0], zin.at[q, 1], zin.at[q, 2]):
                pre = pre + term[at, :].astype(F32)
            sigma = jax.nn.sigmoid(pre)
            layerp[q, at, :] = pre * sigma
            slope = sigma * (1.0 + pre * (1.0 - sigma))
            grows[q, here, b] = (cotp[q, at, :] * slope).astype(BF16)
            return carry

        lax.fori_loop(0, 8, finish, 0)
        for j in (1, 3, 2):
            sends.start(block(q, 0, 0), block(q, 0, 0), gz_sems.at[q, j - 1], along[j])

    def layer():
        def go(b, carry):
            at = pl.ds(pl.multiple_of(b * 64, 64), 64)
            value = unpack(layerp[0, at, :], layerp[1, at, :])
            layer_ref[pl.ds(pl.multiple_of(b * 128, 128), 128), :] = value.astype(BF16)
            return carry

        lax.fori_loop(0, 8, go, 0)

    def near(q, j):
        src = block(q, j, 0)
        if j:
            arrived(src, gz_sems.at[q, j - 1], along[4 - j])
        sends.start(src, src, gnear_sems.at[q, j, 0], right)
        sends.start(src, src, gnear_sems.at[q, j, 1], left)
        sends.start(src, src, gsib_sems.at[q, j, 0], sibling)

    def far(q, j):
        arrived(block(q, j, 3), gnear_sems.at[q, j, 0], left)
        sends.start(block(q, j, 3, 0), block(q, j, 3, 0), gfar_sems.at[q, j, 0], right)
        arrived(block(q, j, 1), gnear_sems.at[q, j, 1], right)
        sends.start(block(q, j, 1, 1), block(q, j, 1, 1), gfar_sems.at[q, j, 1], left)
        sends.start(block(q, j, 3), block(q, j, 3), gsib_sems.at[q, j, 1], sibling)
        sends.start(block(q, j, 1), block(q, j, 1), gsib_sems.at[q, j, 2], sibling)

    def share(q, j):
        arrived(block(q, j, 2, 0), gfar_sems.at[q, j, 0], left)
        sends.start(block(q, j, 2, 0), block(q, j, 2, 0), gsib_sems.at[q, j, 3], sibling)
        arrived(block(q, j, 2, 1), gfar_sems.at[q, j, 1], right)
        sends.start(block(q, j, 2, 1), block(q, j, 2, 1), gsib_sems.at[q, j, 4], sibling)

    def mult(q, j, m):
        if m == 2:
            arrived(block(q, j, 2, 0, 1 - k), gsib_sems.at[q, j, 3], sibling)
            arrived(block(q, j, 2, 1, 1 - k), gsib_sems.at[q, j, 4], sibling)
        else:
            arrived(block(q, j, m, None, 1 - k), gsib_sems.at[q, j, {0: 0, 3: 1, 1: 2}[m]], sibling)

        def go(i, carry):
            c = place_of(j, m, i)
            stage[...] = grows[q, c]
            for n in range(4):
                entry = c * 4 + n
                part = stage[table_ref[1, entry]].astype(F32)
                other = swap(part)
                part = jnp.concatenate(
                    [jnp.concatenate([part, other], axis=1), jnp.concatenate([other, part], axis=1)], axis=0
                ).astype(BF16)
                value = lax.dot_general(
                    tiles[table_ref[0, entry]], part, (((0,), (0,)), ((), ())), preferred_element_type=F32
                )
                prods[q, entry] = jnp.where(lower(64), value[:64, :128], value[64:, 128:])
            return carry

        lax.fori_loop(0, 2, go, 0)

    def add_up(q):
        run[0] = prods[q, table_ref[3, 0]]

        def go(p, carry):
            run[p] = prods[q, table_ref[3, p]] + jnp.where(table_ref[4, p] == 1, run[p - 1], 0.0)
            return carry

        lax.fori_loop(1, 64, go, 0)

        def place_block(r, carry):
            for b in range(8):
                back[q, r, b] = run[table_ref[5, r * 8 + b]].astype(BF16)
            return carry

        lax.fori_loop(0, 8, place_block, 0)

    def dest(m, p):
        return ((y + m) % 4) * 2 + (zh if PIECES[p][0] else 1 - zh)

    def mine_of(q, m, p, part=None):
        _, start, size = PIECES[p]
        if part is not None:
            size = size // 2
            start = start + part * size
        return back.at[q, dest(m, p), pl.ds(start, size)]

    def t1_of(q, p, side):
        return t1.at[q, p, side, pl.ds(0, PIECES[p][2] // 2)]

    def t2_of(q, p, side):
        return t2.at[q, p, side, pl.ds(0, PIECES[p][2])]

    def row_a(q, p):
        sends.start(mine_of(q, 2, p, 0), t1_of(q, p, 0), t1_sems.at[q, p, 0], above)
        sends.start(mine_of(q, 2, p, 1), t1_of(q, p, 1), t1_sems.at[q, p, 1], below)

    def row_b(q, p):
        for m, side, target, source in ((1, 0, above, below), (3, 1, below, above)):
            arrived(t1_of(q, p, side), t1_sems.at[q, p, side], source)
            add_blocks(mine_of(q, m, p, side), [t1_of(q, p, side)], PIECES[p][2] // 2)
            sends.start(mine_of(q, m, p), t2_of(q, p, side), t2_sems.at[q, p, side], target)

    def row_c(q, p):
        arrived(t2_of(q, p, 0), t2_sems.at[q, p, 0], below)
        arrived(t2_of(q, p, 1), t2_sems.at[q, p, 1], above)
        if PIECES[p][0] == 0:
            add_blocks(mine_of(q, 0, p), [t2_of(q, p, 0), t2_of(q, p, 1)], PIECES[p][2])
            _, start, size = PIECES[p]
            sends.start(mine_of(q, 0, p), tz.at[q, pl.ds(start, size)], tz_sems.at[q, p], over)

    def row_end(q):
        for p in range(4):
            _, start, size = PIECES[p]
            arrived(tz.at[q, pl.ds(start, size)], tz_sems.at[q, p], over)
        for p in (4, 5):
            _, start, size = PIECES[p]

            def go(b, carry):
                value = back[q, dest(0, p), start + b].astype(F32) + tz[q, start + b].astype(F32)
                gpp[q, start + b] = value + t2[q, p, 0, b].astype(F32) + t2[q, p, 1, b].astype(F32)
                return carry

            lax.fori_loop(0, size, go, 0)

    eight = [None] + [device((x + i) % 4, y, zh, zl, (k + i // 4) % 2) for i in range(1, 8)]

    def back_of(i):
        return i // 4 * 4 + (4 - i % 4) % 4

    def part_of(i):
        return pl.ds(((k + i // 4) % 2) * 64 + ((x + i) % 4) * GROW, GROW)

    slice_ = part_of(0)

    def turn(part):
        def go(i, carry):
            b = part * 4 + i
            one = xv[b // 4, (b % 4) * 2].astype(F32).T
            two = xv[b // 4, (b % 4) * 2 + 1].astype(F32).T
            low = lower(128)
            xt[b, :128] = jnp.where(low, one, swap(two)).astype(BF16)
            xt[b, 128:] = jnp.where(low, swap(one), two).astype(BF16)
            return carry

        lax.fori_loop(0, 4, go, 0)

    def weight_grad(q):
        total = jnp.zeros((256, 128), F32)
        for b in range(32):
            nodes = back[q, b // 4, pl.ds((b % 4) * 2, 2)].reshape(128, 128)
            total = total + jnp.dot(xt[b], nodes, preferred_element_type=F32)
        gacc[q] = jnp.where(lower(128), total[:128] + swap(total[128:]), 0.0)

    def weight_x():
        gpart[...] = gacc[0] + swap(gacc[1])
        for i in range(8):
            if i:
                sends.start(gpart.at[part_of(i)], g8.at[i], wx_sems.at[i], eight[i])

    def weight_y():
        total = gpart[slice_, :]
        for i in range(1, 8):
            arrived(g8.at[i], wx_sems.at[i], eight[back_of(i)])
            total = total + g8[i]
        g8[0] = total
        for i in range(1, 4):
            sends.start(g8.at[0], gy4.at[i], wy_sems.at[i], ys[i])

    def weight_z():
        for i in range(1, 4):
            arrived(gy4.at[i], wy_sems.at[i], ys[4 - i])
        gy4[0] = g8[0] + gy4[1] + gy4[2] + gy4[3]
        for i in range(1, 8):
            sends.start(gy4.at[0], gz8.at[i], wz_sems.at[i], zs[i])

    def weight_share():
        for i in range(1, 8):
            arrived(gz8.at[i], wz_sems.at[i], zs[8 - i])
        total = gy4[0]
        for i in range(1, 8):
            total = total + gz8[i]
        final[slice_, :] = total
        for i in range(1, 8):
            sends.start(final.at[slice_], final.at[slice_], wg_sems.at[i], eight[i])

    steps = {
        "gz": gather_z, "gown": gather_own, "gnear": gather_near, "gfar": gather_far,
        "gdone": gather_done, "a": step_a, "b": step_b, "c": step_c, "end": end, "near": near, "far": far, "share": share, "mult": mult,
        "sum": add_up, "ra": row_a, "rb": row_b, "rc": row_c, "fin": row_end, "layer": layer,
        "turn": turn, "wg": weight_grad, "wx": weight_x, "wy": weight_y, "wz": weight_z, "ws": weight_share,
    }
    for name, *which in ORDER:
        steps[name](*which)
    row_end(1)
    weight = w_ref[...]

    def output(b, carry):
        value = unpack(gpp[0, b], gpp[1, b])
        high = value.astype(BF16)
        low = (value - high.astype(F32)).astype(BF16)
        dims = (((1,), (1,)), ((), ()))
        result = lax.dot_general(high, weight, dims, preferred_element_type=F32)
        result = result + lax.dot_general(low, weight, dims, preferred_element_type=F32)
        gx_ref[pl.ds(pl.multiple_of(b * 128, 128), 128), :] = result.astype(BF16)
        return carry

    lax.fori_loop(0, 8, output, 0)
    for i in range(1, 8):
        arrived(final.at[part_of(back_of(i))], wg_sems.at[i], eight[back_of(i)])
    gw_ref[...] = final[...]
    sends.finish()


def main(table, x, weight, tiles, cotangent):
    smem, vmem, anywhere = (pl.BlockSpec(memory_space=m) for m in (pltpu.SMEM, pltpu.VMEM, pl.ANY))
    dma = pltpu.SemaphoreType.DMA
    n = len(PIECES)
    return pl.pallas_call(
        main_kernel,
        out_shape=(
            jax.ShapeDtypeStruct((ROWS, 128), BF16),
            jax.ShapeDtypeStruct((ROWS, 128), BF16),
            jax.ShapeDtypeStruct((128, 128), F32),
        ),
        in_specs=[smem, anywhere, vmem, anywhere, vmem],
        out_specs=(vmem, vmem, vmem),
        scratch_shapes=[
            pltpu.VMEM((8, 8, 128, 128), BF16),
            pltpu.VMEM((64, 128, 256), BF16),
            pltpu.VMEM((65, 128, 128), BF16),
            pltpu.VMEM((2, 5, 2, 64, 128), BF16),
            pltpu.VMEM((2, 2, 4, 4, HALF, 128), BF16),
            pltpu.VMEM((2, 4, 4, HALF, 128), BF16),
            pltpu.VMEM((2, 4, 2, QUARTER, 128), BF16),
            pltpu.VMEM((2, 4, 2, HALF, 128), BF16),
            pltpu.VMEM((2, 3, HALF, 128), BF16),
            pltpu.VMEM((2, HALF, 128), F32),
            pltpu.VMEM((2, HALF, 128), F32),
            pltpu.VMEM((2, 32, 8, 64, 128), BF16),
            pltpu.VMEM((8, 64, 128), BF16),
            pltpu.VMEM((2, 128, 64, 128), F32),
            pltpu.VMEM((65, 64, 128), F32),
            pltpu.VMEM((2, 8, 8, 64, 128), BF16),
            pltpu.VMEM((2, n, 2, 2, 64, 128), BF16),
            pltpu.VMEM((2, n, 2, 4, 64, 128), BF16),
            pltpu.VMEM((2, 8, 64, 128), BF16),
            pltpu.VMEM((2, 8, 64, 128), F32),
            pltpu.VMEM((32, 256, 128), BF16),
            pltpu.VMEM((2, 128, 128), F32),
            pltpu.VMEM((8, GROW, 128), F32),
            pltpu.VMEM((4, GROW, 128), F32),
            pltpu.VMEM((8, GROW, 128), F32),
            pltpu.VMEM((128, 128), F32),
            pltpu.VMEM((128, 128), F32),
            dma((2,)), dma((6,)), dma((6, 2)), dma((6, 2)), dma((4, 4, 2)), dma((2, 4, 2)), dma((2, 4, 2)), dma((2, 3)), dma((320,)),
            dma((2, 3)), dma((2, 4, 2)), dma((2, 4, 2)), dma((2, 4, 5)),
            dma((2, n, 2)), dma((2, n, 2)), dma((2, n)),
            dma((8,)), dma((4,)), dma((8,)), dma((8,)),
        ],
        compiler_params=pltpu.CompilerParams(
            collective_id=2, has_side_effects=True, vmem_limit_bytes=VMEM_BYTES
        ),
    )(table, x, weight, tiles, cotangent)


def shards(features, weight, tile_values, tile_rows, tile_cols, tile_live, cotangent):
    table = make_table(tile_live[0], tile_rows[0], tile_cols[0])
    return main(table, features.reshape(8, 128, 128), weight, tile_values[0, 0], cotangent)


def solution(mesh):
    in_specs = (
        P(("col", "row"), None),
        P(),
        P("row", "col", None, None, None),
        P("row", "col", None),
        P("row", "col", None),
        P("row", "col"),
        P(("row", "col"), None),
    )
    out_specs = (P(("row", "col"), None), P(("col", "row"), None), P())
    return jax.shard_map(shards, mesh=mesh, in_specs=in_specs, out_specs=out_specs, check_vma=False)
```

```python
import functools

import jax
import jax.numpy as jnp
from jax import lax
from jax.experimental import pallas as pl
from jax.experimental.pallas import tpu as pltpu
from jax.sharding import PartitionSpec as P

MESH = pl.DeviceIdType.MESH
F32 = jnp.float32
BF16 = jnp.bfloat16
ROWS = 1024
VMEM_BYTES = 56 << 20


def place():
    r, c = lax.axis_index("row"), lax.axis_index("col")
    return (c // 2) % 4, r // 2, r % 2, c // 8, c % 2


def device(x, y, zh, zl, k):
    return (y * 2 + zh, zl * 8 + x * 2 + k)


def remote(src, dst, send, recv, target):
    return pltpu.make_async_remote_copy(
        src_ref=src, dst_ref=dst, send_sem=send, recv_sem=recv, device_id=target, device_id_type=MESH
    )


def greet(partners):
    barrier = pltpu.get_barrier_semaphore()
    for partner in partners:
        pl.semaphore_signal(barrier, inc=1, device_id=partner, device_id_type=MESH)


def greeted(partners):
    pl.semaphore_wait(pltpu.get_barrier_semaphore(), len(partners))


class Sends:
    def __init__(self, send_sems):
        self.sems = send_sems
        self.started = []

    def start(self, src, dst, recv, target):
        copy = remote(src, dst, self.sems.at[len(self.started)], recv, target)
        copy.start()
        self.started.append(copy)

    def finish(self):
        for copy in self.started:
            copy.wait_send()


def arrived(ref, recv, me):
    remote(ref, ref, recv, recv, me).wait_recv()


def each_chunk(rows, step, body):
    def go(i, carry):
        body(pl.ds(pl.multiple_of(i * step, step), step))
        return carry

    lax.fori_loop(0, rows // step, go, 0)


def add_into(out, terms, rows, step=128):
    def body(at):
        total = out[at, :].astype(F32)
        for term in terms:
            total = total + term[at, :].astype(F32)
        out[at, :] = total.astype(out.dtype)

    each_chunk(rows, step, body)


def slot_table(rows, cols, live):
    slots = rows.shape[1]
    i = lax.broadcasted_iota(jnp.int32, (slots, slots), 0)
    lane = lax.broadcasted_iota(jnp.int32, (slots, slots), 1)
    alive = lane < live

    def upright(v):
        return jnp.sum(jnp.where(i == lane, v, 0.0), axis=1, keepdims=True)

    def number(condition, axis=1):
        return jnp.sum(jnp.where(condition, 1.0, 0.0), axis=axis, keepdims=True)

    owner = jnp.floor(rows * 0.125)
    owner_up, rows_up, cols_up = upright(owner), upright(rows), upright(cols)
    rank = number(alive & (owner == owner_up) & ((rows < rows_up) | ((rows == rows_up) & (lane < i))))
    same_row = number(alive & (rows == rows_up) & (lane < i))
    position = number(alive & ((cols < cols_up) | ((cols == cols_up) & (lane < i))))
    same_col = number(alive & (cols == cols_up) & (lane < i))
    slot = lax.broadcasted_iota(jnp.int32, (slots, 128), 0)
    entry = lax.broadcasted_iota(jnp.int32, (slots, 128), 1).astype(F32)
    chosen = jnp.where((owner_up * 4.0 + rank == entry) & (slot < live), 1.0, 0.0)
    placed = jnp.where((position == entry) & (slot < live), 1.0, 0.0)

    def pick(mask, v):
        return jnp.sum(mask * v, axis=0, keepdims=True)

    owners = jnp.where((owner_up == entry) & (slot < live), 1.0, 0.0).astype(BF16)
    offset = rows_up - owner_up * 8.0

    def per_owner(condition):
        ones = jnp.where(condition, 1.0, 0.0).astype(BF16)
        return lax.dot_general(owners, ones, (((0,), (0,)), ((), ())), preferred_element_type=F32)[:32]

    block_count, block_upto = per_owner(offset == entry), per_owner(offset <= entry)
    count = number((cols_up == entry) & (slot < live), 0)
    upto = number((cols_up <= entry) & (slot < live), 0)
    return (
        pick(chosen, slot.astype(F32) - 64.0) + 64.0,
        pick(chosen, rows_up - owner_up * 8.0),
        pick(chosen, cols_up),
        pick(placed, owner_up * 4.0 + rank),
        pick(placed, jnp.where(same_col > 0.0, 1.0, 0.0)),
        jnp.where(count > 0.0, upto - 1.0, 64.0),
        pick(chosen, jnp.where(same_row > 0.0, 1.0, 0.0)),
    ), jnp.where(block_count > 0.0, block_upto - 1.0, 4.0)


def table_kernel(live_ref, rows_ref, cols_ref, table_ref):
    table_ref[...] = jnp.zeros((40, 128), jnp.int32)
    lists, blocks = slot_table(rows_ref[...].astype(F32), cols_ref[...].astype(F32), live_ref[0])
    for n, value in enumerate(lists):
        table_ref[n : n + 1, :] = value.astype(jnp.int32)
    table_ref[8:40, :] = blocks.astype(jnp.int32)


def make_table(live, rows, cols):
    smem, vmem = (pl.BlockSpec(memory_space=m) for m in (pltpu.SMEM, pltpu.VMEM))
    return pl.pallas_call(
        table_kernel,
        out_shape=jax.ShapeDtypeStruct((40, 128), jnp.int32),
        in_specs=[smem, vmem, vmem],
        out_specs=vmem,
    )(live, rows, cols)


HALF = ROWS // 2
QUARTER = ROWS // 4
NEEDED = (
    (2, 2), (1, 2), (3, 2), (2, 1), (2, 3), (0, 2), (1, 1), (1, 3),
    (2, 0), (3, 1), (3, 3), (1, 0), (0, 1), (0, 3), (3, 0), (0, 0),
)
AHEAD = 1
PIECES = ((0, 0, 2), (0, 2, 2), (0, 4, 2), (0, 6, 2), (1, 0, 4), (1, 4, 4))
GROW = 16
GATHER = ((0, 0, 4), (0, 4, 4), (1, 0, 2), (1, 2, 2), (1, 4, 2), (1, 6, 2))
ORDER = (
    ("gz", 2), ("gz", 3), ("gz", 4), ("gz", 5), ("gown",), ("gfar", 0), ("gnear", 2), ("gfar", 1), ("gnear", 3), ("gfar", 2),
    ("gnear", 4), ("gfar", 3), ("gnear", 5), ("gfar", 4), ("gfar", 5), ("gdone",),
    ("a", 0, 2), ("a", 0, 1), ("a", 0, 3), ("b", 0, 2), ("a", 0, 0), ("b", 0, 1), ("a", 1, 2), ("b", 0, 3), ("turn", 0),
    ("c", 0, 2), ("a", 1, 1), ("b", 0, 0), ("c", 0, 1), ("turn", 1), ("a", 1, 3), ("b", 1, 2), ("c", 0, 3), ("turn", 2), ("a", 1, 0),
    ("b", 1, 1), ("c", 0, 0), ("end", 0), ("turn", 3), ("b", 1, 3), ("c", 1, 2), ("turn", 4), ("b", 1, 0), ("near", 0, 0),
    ("c", 1, 1), ("turn", 5), ("near", 0, 1), ("c", 1, 3), ("turn", 6), ("near", 0, 3), ("c", 1, 0), ("end", 1),
    ("far", 0, 0), ("near", 0, 2), ("far", 0, 1), ("near", 1, 0), ("mult", 0, 0, 0), ("turn", 7), ("mult", 0, 1, 0),
    ("far", 0, 3), ("mult", 0, 3, 0), ("near", 1, 1), ("share", 0, 0), ("mult", 0, 0, 3), ("mult", 0, 0, 1),
    ("far", 0, 2), ("near", 1, 3), ("share", 0, 1), ("mult", 0, 1, 3), ("mult", 0, 1, 1), ("mult", 0, 2, 0),
    ("far", 1, 0), ("near", 1, 2), ("share", 0, 3), ("mult", 0, 3, 3), ("mult", 0, 3, 1), ("mult", 0, 0, 2),
    ("far", 1, 1), ("share", 0, 2), ("mult", 0, 2, 3), ("mult", 0, 2, 1), ("mult", 0, 1, 2), ("mult", 0, 3, 2),
    ("mult", 0, 2, 2), ("sum", 0), ("ra", 0, 0), ("ra", 0, 1), ("ra", 0, 2), ("ra", 0, 3),
    ("far", 1, 3), ("share", 1, 0), ("wg", 0), ("mult", 1, 0, 0), ("mult", 1, 1, 0), ("rb", 0, 0), ("rb", 0, 1),
    ("far", 1, 2), ("mult", 1, 3, 0), ("mult", 1, 0, 3), ("rb", 0, 2), ("rb", 0, 3), ("ra", 0, 4), ("ra", 0, 5),
    ("share", 1, 1), ("mult", 1, 0, 1), ("mult", 1, 1, 3), ("mult", 1, 1, 1), ("rc", 0, 0), ("rc", 0, 1),
    ("mult", 1, 2, 0), ("mult", 1, 3, 3), ("mult", 1, 3, 1), ("rc", 0, 2), ("rc", 0, 3),
    ("share", 1, 3), ("mult", 1, 0, 2), ("mult", 1, 1, 2), ("rb", 0, 4), ("rb", 0, 5),
    ("mult", 1, 2, 3), ("mult", 1, 2, 1), ("mult", 1, 3, 2), ("share", 1, 2), ("mult", 1, 2, 2),
    ("sum", 1), ("ra", 1, 0), ("ra", 1, 1), ("ra", 1, 2), ("ra", 1, 3), ("wg", 1), ("wx",),
    ("rb", 1, 0), ("rb", 1, 1), ("rb", 1, 2), ("rb", 1, 3), ("rc", 1, 0), ("wy",), ("rc", 1, 1), ("ra", 1, 4),
    ("ra", 1, 5), ("rc", 1, 2), ("rc", 1, 3), ("wz",), ("rc", 0, 4), ("rc", 0, 5), ("fin", 0), ("layer",),
    ("rb", 1, 4), ("rb", 1, 5), ("ws",), ("rc", 1, 4), ("rc", 1, 5),
)


def swap(value):
    return pltpu.roll(value, 64, 1)


def lower(rows):
    return lax.broadcasted_iota(jnp.int32, (rows, 128), 1) < 64


def pack(value):
    top, bottom = value[:64], value[64:]
    low = lower(64)
    return jnp.where(low, top, swap(bottom)), jnp.where(low, swap(top), bottom)


def unpack(first, second):
    low = lower(64)
    return jnp.concatenate([jnp.where(low, first, swap(second)), jnp.where(low, swap(first), second)], axis=0)


def add_blocks(out, terms, blocks):
    def go(b, carry):
        total = out[b].astype(F32)
        for term in terms:
            total = total + term[b].astype(F32)
        out[b] = total.astype(out.dtype)
        return carry

    lax.fori_loop(0, blocks, go, 0)


def main_kernel(
    table_ref, x_ref, w_ref, tiles_ref, cot_ref, layer_ref, gx_ref, gw_ref,
    xv, proj, tiles, runs, both, sib, s1, s2, zin, cotp, layerp, grows, stage, prods, run, back, t1, t2, tz, gpp,
    xt, gacc, g8, gy4, gz8, gpart, final,
    load_sems, gz_row, gnear_row, gfar_row, sib_sems, s1_sems, s2_sems, z_sems, send_sems, gz_sems, gnear_sems, gfar_sems, gsib_sems,
    t1_sems, t2_sems, tz_sems, wx_sems, wy_sems, wz_sems, wg_sems,
):
    x, y, zh, zl, k = place()
    z = zh * 4 + zl
    sibling = device(x, y, zh, zl, 1 - k)
    xs = [None] + [device((x + i) % 4, y, zh, zl, k) for i in range(1, 4)]
    ys = [None] + [device(x, (y + i) % 4, zh, zl, k) for i in range(1, 4)]
    zs = [None] + [device(x, y, ((z + i) % 8) // 4, ((z + i) % 8) % 4, k) for i in range(1, 8)]
    along = [None] + [device(x, y, zh, (zl + j) % 4, k) for j in range(1, 4)]
    over = device(x, y, 1 - zh, zl, k)
    right, left, above, below = xs[1], xs[3], ys[1], ys[3]
    first, second = pl.ds(0, QUARTER), pl.ds(QUARTER, QUARTER)

    partners = [device((x + i % 4) % 4, y, zh, zl, (k + i // 4) % 2) for i in range(1, 8)] + ys[1:] + zs[1:]
    here_row = y * 2 + zh
    load_x = pltpu.make_async_copy(x_ref, xv.at[here_row], load_sems.at[0])
    load_x.start()
    load_t = pltpu.make_async_copy(tiles_ref, tiles.at[pl.ds(0, 64)], load_sems.at[1])
    load_t.start()
    greet(partners)

    straight = w_ref[...].astype(F32)
    twice = jnp.concatenate([straight, swap(straight)], axis=1).astype(BF16)
    greeted(partners)
    sends = Sends(send_sems)

    def gather_at(yy, p, part=None):
        side, start, size = GATHER[p]
        row = (yy % 4) * 2 + (1 - zh if side else zh)
        if part is not None:
            size = size // 2
            start = start + part * size
        return row, start, size

    def gathered(yy, p, part=None):
        row, start, size = gather_at(yy, p, part)
        return xv.at[row, pl.ds(start, size)]

    def project(yy, p, part=None):
        row, start, size = gather_at(yy, p, part)
        nodes = xv[row, pl.ds(start, size)].reshape(size * 128, 128)
        value = jnp.dot(nodes, twice, preferred_element_type=F32).astype(BF16)
        proj[pl.ds(row * 8 + start, size)] = value.reshape(size, 128, 256)

    def gather_z(p):
        _, start, size = GATHER[p]
        src = x_ref.at[pl.ds(start, size)]
        sends.start(src, xv.at[here_row, pl.ds(start, size)], gz_row.at[p], over)

    def gather_own():
        for p in (0, 1):
            _, start, size = GATHER[p]
            src = x_ref.at[pl.ds(start, size)]
            sends.start(src, gathered(y, p), gnear_row.at[p, 0], above)
            sends.start(src, gathered(y, p), gnear_row.at[p, 1], below)
        tiles[64] = jnp.zeros((128, 128), BF16)
        run[64] = jnp.zeros((64, 128), F32)
        for i in range(2):
            runs[i, 4] = jnp.zeros((2, 64, 128), BF16)
        load_x.wait()
        for p in (0, 1):
            project(y, p)
        load_t.wait()

    def gather_near(p):
        arrived(gathered(y, p), gz_row.at[p], over)
        sends.start(gathered(y, p), gathered(y, p), gnear_row.at[p, 0], above)
        sends.start(gathered(y, p), gathered(y, p), gnear_row.at[p, 1], below)
        project(y, p)

    def gather_far(p):
        arrived(gathered(y + 3, p), gnear_row.at[p, 0], below)
        sends.start(gathered(y + 3, p, 0), gathered(y + 3, p, 0), gfar_row.at[p, 0], above)
        arrived(gathered(y + 1, p), gnear_row.at[p, 1], above)
        sends.start(gathered(y + 1, p, 1), gathered(y + 1, p, 1), gfar_row.at[p, 1], below)
        project(y + 3, p)
        project(y + 1, p)

    def gather_done():
        for p in range(len(GATHER)):
            arrived(gathered(y + 2, p, 0), gfar_row.at[p, 0], below)
            arrived(gathered(y + 2, p, 1), gfar_row.at[p, 1], above)
            project(y + 2, p)

    def produce(j, m):
        def side(i, carry):
            core = (1 - k) + i * (2 * k - 1)
            c = ((zl + j) % 4) * 8 + ((x + m) % 4) * 2 + core
            low = lower(64)
            before = None
            for n in range(4):
                entry = c * 4 + n
                value = jnp.dot(tiles[table_ref[0, entry]], proj[table_ref[2, entry]], preferred_element_type=F32)
                value = (
                    jnp.where(low, value[:64, :128], value[64:, 128:]),
                    jnp.where(low, value[:64, 128:], value[64:, :128]),
                )
                if n:
                    same = table_ref[6, entry] == 1
                    value = tuple(v + jnp.where(same, u, 0.0) for v, u in zip(value, before))
                for q in range(2):
                    runs[i, n, q] = value[q].astype(BF16)
                before = value
            for b in range(8):
                at = table_ref[8 + c, b]
                for q in range(2):
                    both[i, q, j, m, pl.ds(b * 64, 64), :] = runs[i, at, q]
            return carry

        lax.fori_loop(0, 2, side, 0)
        for q in range(2):
            sends.start(both.at[0, q, j, m], sib.at[q, j, m], sib_sems.at[j, m, q], sibling)

    produced = []

    def joined(j, m, q):
        while len(produced) < len(NEEDED) and len(produced) <= NEEDED.index((j, m)) + AHEAD:
            produce(*NEEDED[len(produced)])
            produced.append(True)
        arrived(sib.at[q, j, m], sib_sems.at[j, m, q], sibling)

    def step_a(q, j):
        joined(j, 2, q)
        add_into(both.at[1, q, j, 2], [sib.at[q, j, 2]], HALF)
        sends.start(both.at[1, q, j, 2, first], s1.at[q, j, 0], s1_sems.at[q, j, 0], right)
        sends.start(both.at[1, q, j, 2, second], s1.at[q, j, 1], s1_sems.at[q, j, 1], left)

    def step_b(q, j):
        for m, side, near, far, target, source in ((1, 0, first, second, right, left), (3, 1, second, first, left, right)):
            joined(j, m, q)
            mine = both.at[1, q, j, m]
            add_into(mine.at[far], [sib.at[q, j, m, far]], QUARTER)
            arrived(s1.at[q, j, side], s1_sems.at[q, j, side], source)
            add_into(mine.at[near], [sib.at[q, j, m, near], s1.at[q, j, side]], QUARTER)
            sends.start(mine, s2.at[q, j, side], s2_sems.at[q, j, side], target)

    def step_c(q, j):
        joined(j, 0, q)
        arrived(s2.at[q, j, 0], s2_sems.at[q, j, 0], left)
        arrived(s2.at[q, j, 1], s2_sems.at[q, j, 1], right)
        if j:
            mine = both.at[1, q, j, 0]
            add_into(mine, [sib.at[q, j, 0], s2.at[q, j, 0], s2.at[q, j, 1]], HALF)
            sends.start(mine, zin.at[q, j - 1], z_sems.at[q, j - 1], along[j])

    def place_of(j, m, core):
        return ((zl + 4 - j) % 4) * 8 + ((x + m) % 4) * 2 + core

    def block(q, j, m, part=None, core=None):
        at = grows.at[q, place_of(j, m, k if core is None else core)]
        return at if part is None else at.at[pl.ds(part * 4, 4)]

    def pack_cotangent():
        def go(b, carry):
            value = cot_ref[pl.ds(pl.multiple_of(b * 128, 128), 128), :].astype(F32)
            for q, part in enumerate(pack(value)):
                cotp[q, pl.ds(pl.multiple_of(b * 64, 64), 64), :] = part
            return carry

        lax.fori_loop(0, 8, go, 0)

    def end(q):
        if q == 0:
            pack_cotangent()
        for j in range(1, 4):
            arrived(zin.at[q, j - 1], z_sems.at[q, j - 1], along[4 - j])
        here = place_of(0, 0, k)

        def finish(b, carry):
            at = pl.ds(pl.multiple_of(b * 64, 64), 64)
            pre = both[1, q, 0, 0, at, :].astype(F32) + sib[q, 0, 0, at, :].astype(F32)
            for term in (s2.at[q, 0, 0], s2.at[q, 0, 1], zin.at[q, 0], zin.at[q, 1], zin.at[q, 2]):
                pre = pre + term[at, :].astype(F32)
            sigma = jax.nn.sigmoid(pre)
            layerp[q, at, :] = pre * sigma
            slope = sigma * (1.0 + pre * (1.0 - sigma))
            grows[q, here, b] = (cotp[q, at, :] * slope).astype(BF16)
            return carry

        lax.fori_loop(0, 8, finish, 0)
        for j in (1, 3, 2):
            sends.start(block(q, 0, 0), block(q, 0, 0), gz_sems.at[q, j - 1], along[j])

    def layer():
        def go(b, carry):
            at = pl.ds(pl.multiple_of(b * 64, 64), 64)
            value = unpack(layerp[0, at, :], layerp[1, at, :])
            layer_ref[pl.ds(pl.multiple_of(b * 128, 128), 128), :] = value.astype(BF16)
            return carry

        lax.fori_loop(0, 8, go, 0)

    def near(q, j):
        src = block(q, j, 0)
        if j:
            arrived(src, gz_sems.at[q, j - 1], along[4 - j])
        sends.start(src, src, gnear_sems.at[q, j, 0], right)
        sends.start(src, src, gnear_sems.at[q, j, 1], left)
        sends.start(src, src, gsib_sems.at[q, j, 0], sibling)

    def far(q, j):
        arrived(block(q, j, 3), gnear_sems.at[q, j, 0], left)
        sends.start(block(q, j, 3, 0), block(q, j, 3, 0), gfar_sems.at[q, j, 0], right)
        arrived(block(q, j, 1), gnear_sems.at[q, j, 1], right)
        sends.start(block(q, j, 1, 1), block(q, j, 1, 1), gfar_sems.at[q, j, 1], left)
        sends.start(block(q, j, 3), block(q, j, 3), gsib_sems.at[q, j, 1], sibling)
        sends.start(block(q, j, 1), block(q, j, 1), gsib_sems.at[q, j, 2], sibling)

    def share(q, j):
        arrived(block(q, j, 2, 0), gfar_sems.at[q, j, 0], left)
        sends.start(block(q, j, 2, 0), block(q, j, 2, 0), gsib_sems.at[q, j, 3], sibling)
        arrived(block(q, j, 2, 1), gfar_sems.at[q, j, 1], right)
        sends.start(block(q, j, 2, 1), block(q, j, 2, 1), gsib_sems.at[q, j, 4], sibling)

    def mult(q, j, m):
        if m == 2:
            arrived(block(q, j, 2, 0, 1 - k), gsib_sems.at[q, j, 3], sibling)
            arrived(block(q, j, 2, 1, 1 - k), gsib_sems.at[q, j, 4], sibling)
        else:
            arrived(block(q, j, m, None, 1 - k), gsib_sems.at[q, j, {0: 0, 3: 1, 1: 2}[m]], sibling)

        def go(i, carry):
            c = place_of(j, m, i)
            stage[...] = grows[q, c]
            for n in range(4):
                entry = c * 4 + n
                part = stage[table_ref[1, entry]].astype(F32)
                other = swap(part)
                part = jnp.concatenate(
                    [jnp.concatenate([part, other], axis=1), jnp.concatenate([other, part], axis=1)], axis=0
                ).astype(BF16)
                value = lax.dot_general(
                    tiles[table_ref[0, entry]], part, (((0,), (0,)), ((), ())), preferred_element_type=F32
                )
                prods[q, entry] = jnp.where(lower(64), value[:64, :128], value[64:, 128:])
            return carry

        lax.fori_loop(0, 2, go, 0)

    def add_up(q):
        run[0] = prods[q, table_ref[3, 0]]

        def go(p, carry):
            run[p] = prods[q, table_ref[3, p]] + jnp.where(table_ref[4, p] == 1, run[p - 1], 0.0)
            return carry

        lax.fori_loop(1, 64, go, 0)

        def place_block(r, carry):
            for b in range(8):
                back[q, r, b] = run[table_ref[5, r * 8 + b]].astype(BF16)
            return carry

        lax.fori_loop(0, 8, place_block, 0)

    def dest(m, p):
        return ((y + m) % 4) * 2 + (zh if PIECES[p][0] else 1 - zh)

    def mine_of(q, m, p, part=None):
        _, start, size = PIECES[p]
        if part is not None:
            size = size // 2
            start = start + part * size
        return back.at[q, dest(m, p), pl.ds(start, size)]

    def t1_of(q, p, side):
        return t1.at[q, p, side, pl.ds(0, PIECES[p][2] // 2)]

    def t2_of(q, p, side):
        return t2.at[q, p, side, pl.ds(0, PIECES[p][2])]

    def row_a(q, p):
        sends.start(mine_of(q, 2, p, 0), t1_of(q, p, 0), t1_sems.at[q, p, 0], above)
        sends.start(mine_of(q, 2, p, 1), t1_of(q, p, 1), t1_sems.at[q, p, 1], below)

    def row_b(q, p):
        for m, side, target, source in ((1, 0, above, below), (3, 1, below, above)):
            arrived(t1_of(q, p, side), t1_sems.at[q, p, side], source)
            add_blocks(mine_of(q, m, p, side), [t1_of(q, p, side)], PIECES[p][2] // 2)
            sends.start(mine_of(q, m, p), t2_of(q, p, side), t2_sems.at[q, p, side], target)

    def row_c(q, p):
        arrived(t2_of(q, p, 0), t2_sems.at[q, p, 0], below)
        arrived(t2_of(q, p, 1), t2_sems.at[q, p, 1], above)
        if PIECES[p][0] == 0:
            add_blocks(mine_of(q, 0, p), [t2_of(q, p, 0), t2_of(q, p, 1)], PIECES[p][2])
            _, start, size = PIECES[p]
            sends.start(mine_of(q, 0, p), tz.at[q, pl.ds(start, size)], tz_sems.at[q, p], over)

    def row_end(q):
        for p in range(4):
            _, start, size = PIECES[p]
            arrived(tz.at[q, pl.ds(start, size)], tz_sems.at[q, p], over)
        for p in (4, 5):
            _, start, size = PIECES[p]

            def go(b, carry):
                value = back[q, dest(0, p), start + b].astype(F32) + tz[q, start + b].astype(F32)
                gpp[q, start + b] = value + t2[q, p, 0, b].astype(F32) + t2[q, p, 1, b].astype(F32)
                return carry

            lax.fori_loop(0, size, go, 0)

    eight = [None] + [device((x + i) % 4, y, zh, zl, (k + i // 4) % 2) for i in range(1, 8)]

    def back_of(i):
        return i // 4 * 4 + (4 - i % 4) % 4

    def part_of(i):
        return pl.ds(((k + i // 4) % 2) * 64 + ((x + i) % 4) * GROW, GROW)

    slice_ = part_of(0)

    def turn(part):
        def go(i, carry):
            b = part * 4 + i
            one = xv[b // 4, (b % 4) * 2].astype(F32).T
            two = xv[b // 4, (b % 4) * 2 + 1].astype(F32).T
            low = lower(128)
            xt[b, :128] = jnp.where(low, one, swap(two)).astype(BF16)
            xt[b, 128:] = jnp.where(low, swap(one), two).astype(BF16)
            return carry

        lax.fori_loop(0, 4, go, 0)

    def weight_grad(q):
        total = jnp.zeros((256, 128), F32)
        for b in range(32):
            nodes = back[q, b // 4, pl.ds((b % 4) * 2, 2)].reshape(128, 128)
            total = total + jnp.dot(xt[b], nodes, preferred_element_type=F32)
        gacc[q] = jnp.where(lower(128), total[:128] + swap(total[128:]), 0.0)

    def weight_x():
        gpart[...] = gacc[0] + swap(gacc[1])
        for i in range(8):
            if i:
                sends.start(gpart.at[part_of(i)], g8.at[i], wx_sems.at[i], eight[i])

    def weight_y():
        total = gpart[slice_, :]
        for i in range(1, 8):
            arrived(g8.at[i], wx_sems.at[i], eight[back_of(i)])
            total = total + g8[i]
        g8[0] = total
        for i in range(1, 4):
            sends.start(g8.at[0], gy4.at[i], wy_sems.at[i], ys[i])

    def weight_z():
        for i in range(1, 4):
            arrived(gy4.at[i], wy_sems.at[i], ys[4 - i])
        gy4[0] = g8[0] + gy4[1] + gy4[2] + gy4[3]
        for i in range(1, 8):
            sends.start(gy4.at[0], gz8.at[i], wz_sems.at[i], zs[i])

    def weight_share():
        for i in range(1, 8):
            arrived(gz8.at[i], wz_sems.at[i], zs[8 - i])
        total = gy4[0]
        for i in range(1, 8):
            total = total + gz8[i]
        final[slice_, :] = total
        for i in range(1, 8):
            sends.start(final.at[slice_], final.at[slice_], wg_sems.at[i], eight[i])

    steps = {
        "gz": gather_z, "gown": gather_own, "gnear": gather_near, "gfar": gather_far,
        "gdone": gather_done, "a": step_a, "b": step_b, "c": step_c, "end": end, "near": near, "far": far, "share": share, "mult": mult,
        "sum": add_up, "ra": row_a, "rb": row_b, "rc": row_c, "fin": row_end, "layer": layer,
        "turn": turn, "wg": weight_grad, "wx": weight_x, "wy": weight_y, "wz": weight_z, "ws": weight_share,
    }
    for name, *which in ORDER:
        steps[name](*which)
    row_end(1)
    weight = w_ref[...]

    def output(b, carry):
        value = unpack(gpp[0, b], gpp[1, b])
        high = value.astype(BF16)
        low = (value - high.astype(F32)).astype(BF16)
        dims = (((1,), (1,)), ((), ()))
        result = lax.dot_general(high, weight, dims, preferred_element_type=F32)
        result = result + lax.dot_general(low, weight, dims, preferred_element_type=F32)
        gx_ref[pl.ds(pl.multiple_of(b * 128, 128), 128), :] = result.astype(BF16)
        return carry

    lax.fori_loop(0, 8, output, 0)
    for i in range(1, 8):
        arrived(final.at[part_of(back_of(i))], wg_sems.at[i], eight[back_of(i)])
    gw_ref[...] = final[...]
    sends.finish()


def main(table, x, weight, tiles, cotangent):
    smem, vmem, anywhere = (pl.BlockSpec(memory_space=m) for m in (pltpu.SMEM, pltpu.VMEM, pl.ANY))
    dma = pltpu.SemaphoreType.DMA
    n = len(PIECES)
    return pl.pallas_call(
        main_kernel,
        out_shape=(
            jax.ShapeDtypeStruct((ROWS, 128), BF16),
            jax.ShapeDtypeStruct((ROWS, 128), BF16),
            jax.ShapeDtypeStruct((128, 128), F32),
        ),
        in_specs=[smem, anywhere, vmem, anywhere, vmem],
        out_specs=(vmem, vmem, vmem),
        scratch_shapes=[
            pltpu.VMEM((8, 8, 128, 128), BF16),
            pltpu.VMEM((64, 128, 256), BF16),
            pltpu.VMEM((65, 128, 128), BF16),
            pltpu.VMEM((2, 5, 2, 64, 128), BF16),
            pltpu.VMEM((2, 2, 4, 4, HALF, 128), BF16),
            pltpu.VMEM((2, 4, 4, HALF, 128), BF16),
            pltpu.VMEM((2, 4, 2, QUARTER, 128), BF16),
            pltpu.VMEM((2, 4, 2, HALF, 128), BF16),
            pltpu.VMEM((2, 3, HALF, 128), BF16),
            pltpu.VMEM((2, HALF, 128), F32),
            pltpu.VMEM((2, HALF, 128), F32),
            pltpu.VMEM((2, 32, 8, 64, 128), BF16),
            pltpu.VMEM((8, 64, 128), BF16),
            pltpu.VMEM((2, 128, 64, 128), F32),
            pltpu.VMEM((65, 64, 128), F32),
            pltpu.VMEM((2, 8, 8, 64, 128), BF16),
            pltpu.VMEM((2, n, 2, 2, 64, 128), BF16),
            pltpu.VMEM((2, n, 2, 4, 64, 128), BF16),
            pltpu.VMEM((2, 8, 64, 128), BF16),
            pltpu.VMEM((2, 8, 64, 128), F32),
            pltpu.VMEM((32, 256, 128), BF16),
            pltpu.VMEM((2, 128, 128), F32),
            pltpu.VMEM((8, GROW, 128), F32),
            pltpu.VMEM((4, GROW, 128), F32),
            pltpu.VMEM((8, GROW, 128), F32),
            pltpu.VMEM((128, 128), F32),
            pltpu.VMEM((128, 128), F32),
            dma((2,)), dma((6,)), dma((6, 2)), dma((6, 2)), dma((4, 4, 2)), dma((2, 4, 2)), dma((2, 4, 2)), dma((2, 3)), dma((320,)),
            dma((2, 3)), dma((2, 4, 2)), dma((2, 4, 2)), dma((2, 4, 5)),
            dma((2, n, 2)), dma((2, n, 2)), dma((2, n)),
            dma((8,)), dma((4,)), dma((8,)), dma((8,)),
        ],
        compiler_params=pltpu.CompilerParams(
            collective_id=2, has_side_effects=True, vmem_limit_bytes=VMEM_BYTES
        ),
    )(table, x, weight, tiles, cotangent)


def hand_over_kernel(*refs):
    sems = refs[6]
    copies = [pltpu.make_async_copy(refs[i], refs[3 + i], sems.at[i]) for i in range(3)]
    for copy in copies:
        copy.start()
    for copy in copies:
        copy.wait()


def hand_over(*results):
    anywhere = pl.BlockSpec(memory_space=pl.ANY)
    return pl.pallas_call(
        hand_over_kernel,
        out_shape=tuple(jax.ShapeDtypeStruct(v.shape, v.dtype) for v in results),
        in_specs=[anywhere] * 3,
        out_specs=(anywhere,) * 3,
        scratch_shapes=[pltpu.SemaphoreType.DMA((3,))],
    )(*results)


def shards(features, weight, tile_values, tile_rows, tile_cols, tile_live, cotangent):
    table = make_table(tile_live[0], tile_rows[0], tile_cols[0])
    return hand_over(*main(table, features.reshape(8, 128, 128), weight, tile_values[0, 0], cotangent))


def solution(mesh):
    in_specs = (
        P(("col", "row"), None),
        P(),
        P("row", "col", None, None, None),
        P("row", "col", None),
        P("row", "col", None),
        P("row", "col"),
        P(("row", "col"), None),
    )
    out_specs = (P(("row", "col"), None), P(("col", "row"), None), P())
    return jax.shard_map(shards, mesh=mesh, in_specs=in_specs, out_specs=out_specs, check_vma=False)
```
